128 devices in a mesh: ctx: 16 (over z, y_lo, core), head: 2 (over y_hi), dp: 4 (over x).
Axes of the slice: x: 4, y: 4 (y_hi: 2, y_lo: 2; y = y_hi * 2 + y_lo), z: 4, core: 2. Of those that a mesh axis runs over, the one named last changes fastest.
Arguments:
- queries: bfloat16 [4, 8192, 1024], P('dp', 'ctx', 'head'), may hold values from -4.5 to 4.5
- key_vectors: bfloat16 [4, 8192, 1024], P('dp', 'ctx', 'head'), may hold values from -4.5 to 4.5
- value_vectors: bfloat16 [4, 8192, 1024], P('dp', 'ctx', 'head'), may hold values from -18 to 18
- cotangent: bfloat16 [4, 8192, 2048], P('dp', 'ctx', 'head'), may hold values from -6 to 6
- w_out: bfloat16 [1024, 2048], P('head'), may hold values from -0.1875 to 0.1875
- phoneme_keys: bfloat16 [4, 256, 1024], P('dp', None, 'head'), may hold values from -5 to 5
- phoneme_values: bfloat16 [4, 256, 1024], P('dp', None, 'head'), may hold values from -18 to 18
- phrase_blocks: int32 [4, 64, 4], P('dp'), may hold values from 0 to 63, as said below
- phrase_count: int32 [4, 64], P('dp', 'ctx'), may hold values from 0 to 4, as said below
- alignment: int32 [4, 8192], P('dp', 'ctx'), may hold values from 0 to 255, as said below
Outputs:
- layer_out: bfloat16 [4, 8192, 2048], P('dp', 'ctx', 'head')
- d_queries: bfloat16 [4, 8192, 1024], P('dp', 'ctx', 'head')
- d_keys: bfloat16 [4, 8192, 1024], P('dp', 'ctx', 'head')
- d_values: bfloat16 [4, 8192, 1024], P('dp', 'ctx', 'head')
- d_phoneme_keys: bfloat16 [4, 256, 1024], P('dp', None, 'head')
- d_phoneme_values: bfloat16 [4, 256, 1024], P('dp', None, 'head')
- d_w_out: float32 [1024, 2048], P('head', ('ctx', 'dp'))
The draws below stay inside these ranges and needn't reach their ends.
Inputs may be any that keep to these rules, and one draw needn't show every extreme that they name: `phrase_blocks`: block j lies on index j // 4 of ctx. Every entry names a block on another index than its query block; all entries of the query blocks of one index that lie on the same other index name the same block; no entry names the first block of the next index or the last block of the previous index. `phrase_count`: the first query block of every index of ctx has all 4 slots in use. alignment[b, t] lies within 2 of t * 256 // 8192; the first frame is aligned to phoneme 0 and the last to phoneme 256 - 1.
All inputs are finite; a program needn't handle non-finite values.
Results may differ from the reference program's by a relative error of at most 0.018.
Values may be sent and summed in bfloat16 or wider, within the bound.
A program may use at most 128 MiB of HBM per device.

```python
import math
import jax
import jax.numpy as jnp
from jax import lax

D = 2048
DH = 128
BLK = 128
HALF_BAND = 64
PHRASE_SLOTS = 4
PH_HALF = 16
F_DEV = 512
PH = 256
HD = 1024
SEQ = 8192
NBLK = 64
BATCH = 4
N_CTX = 16


def draw_queries(key, part):
    own_key = jax.random.fold_in(key, 1)
    result = jnp.clip(jax.random.normal(own_key, (BATCH, SEQ, HD)), -4.5, 4.5)
    return result.astype(jnp.bfloat16)


def draw_key_vectors(key, part):
    own_key = jax.random.fold_in(key, 2)
    result = jnp.clip(jax.random.normal(own_key, (BATCH, SEQ, HD)), -4.5, 4.5)
    return result.astype(jnp.bfloat16)


def draw_phrase_blocks(key, part):
    per_dev = F_DEV // BLK
    ctx_count = NBLK // per_dev
    first_key, second_key, third_key, fourth_key = jax.random.split(key, 4)
    draw_shape = (BATCH, ctx_count, ctx_count)
    any_block = jax.random.randint(first_key, draw_shape, 0, per_dev)
    after_first = jax.random.randint(second_key, draw_shape, 1, per_dev)
    before_last = jax.random.randint(third_key, draw_shape, 0, per_dev - 1)
    destination = jnp.arange(ctx_count)[:, None]
    source = jnp.arange(ctx_count)[None, :]
    pool = jnp.where(source == destination + 1, after_first, jnp.where(source == destination - 1, before_last, any_block))
    owner_dev = jnp.arange(NBLK) // per_dev
    offset = jax.random.randint(fourth_key, (BATCH, NBLK, PHRASE_SLOTS), 1, ctx_count)
    source_dev = (owner_dev[None, :, None] + offset) % ctx_count
    pool_rows = pool[:, owner_dev, :]
    chosen = jnp.take_along_axis(pool_rows, source_dev, axis=2)
    return (source_dev * per_dev + chosen).astype(jnp.int32)


def draw_phrase_count(key, part):
    per_dev = F_DEV // BLK
    counts = jax.random.randint(key, (BATCH, NBLK), 0, PHRASE_SLOTS + 1)
    first_frame_on_device = (jnp.arange(NBLK) % per_dev == 0)[None, :]
    return jnp.where(first_frame_on_device, PHRASE_SLOTS, counts).astype(jnp.int32)


def draw_alignment(key, part):
    frame_ids = jnp.arange(SEQ)
    base_value = frame_ids * PH // SEQ
    jitter = jax.random.randint(key, (BATCH, SEQ), -2, 3)
    result = jnp.clip(base_value[None, :] + jitter, 0, PH - 1)
    result = jnp.where(frame_ids[None, :] == 0, 0, result)
    result = jnp.where(frame_ids[None, :] == SEQ - 1, PH - 1, result)
    return result.astype(jnp.int32)


def strengthened(values, key, source, target, blocks, factor):
    owner, partner = [(jnp.arange(values.shape[dim]) // (values.shape[dim] // blocks)).reshape([-1 if axis == dim else 1 for axis in range(values.ndim)]) for dim in (source, target)]
    chosen = jax.random.permutation(key, blocks)[partner]
    strong = (owner == chosen) | (owner == (partner + blocks // 2) % blocks)
    return jnp.where(strong, factor * values, values)


def levels(key, dims, cuts, smallest, largest):
    loudness = 1.0
    for axis_at, blocks in cuts:
        steps = jax.random.uniform(jax.random.fold_in(jax.random.fold_in(key, 6), axis_at), (blocks,), jnp.float32, smallest / len(cuts), largest / len(cuts))
        loudness = loudness * jnp.repeat(jnp.exp(steps), dims[axis_at] // blocks).reshape((-1,) + (1,) * (len(dims) - 1 - axis_at))
    return loudness


def gaussian(key, shape, scale, limit, cuts=(), kind=jnp.bfloat16):
    loudness = levels(key, shape, cuts, -0.22, 0.18) if cuts else 1.0
    values = jax.random.normal(key, shape, jnp.float32) * scale * loudness
    return jnp.minimum(jnp.maximum(values, -limit), limit).astype(kind)


def heavy_noise(key, dims, scale, limit, pieces, heavy, held_as=jnp.bfloat16):
    values = scale * jax.random.normal(key, dims, jnp.float32)
    if pieces:
        values = values * levels(key, dims, pieces, -0.22, 0.18)
    return jnp.clip(strengthened(values, jax.random.fold_in(key, 3), *heavy), -limit, limit).astype(held_as)


def setup_inputs(seed: int = 0) -> dict:
    streams_of = jax.random.split(jax.random.key(seed), 11)
    queries = draw_queries(jax.random.fold_in(streams_of[10], 71), 0)
    key_vectors = draw_key_vectors(jax.random.fold_in(streams_of[10], 71), 0)
    value_vectors = gaussian(streams_of[2], (BATCH, SEQ, HD), 3.0, 18.0, ((0, 4), (1, 16), (2, 2)))
    cotangent = heavy_noise(streams_of[3], (BATCH, SEQ, D), 1.0, 6.0, ((0, 4), (1, 16), (2, 2)), (1, 2, 16, 2.0))
    w_out = gaussian(streams_of[4], (HD, D), HD ** -0.5, 0.1875, ((0, 2),))
    phoneme_keys = gaussian(streams_of[5], (BATCH, PH, HD), 1.0, 5.0, ((0, 4), (2, 2)))
    phoneme_values = gaussian(streams_of[6], (BATCH, PH, HD), 3.0, 18.0, ((0, 4), (2, 2)))
    phrase_blocks = draw_phrase_blocks(jax.random.fold_in(streams_of[10], 71), 0)
    phrase_count = draw_phrase_count(jax.random.fold_in(streams_of[10], 71), 0)
    alignment = draw_alignment(jax.random.fold_in(streams_of[10], 71), 0)
    return {"queries": queries, "key_vectors": key_vectors, "value_vectors": value_vectors, "cotangent": cotangent, "w_out": w_out, "phoneme_keys": phoneme_keys, "phoneme_values": phoneme_values, "phrase_blocks": phrase_blocks, "phrase_count": phrase_count, "alignment": alignment}


masked_score = -1e+30

def round_half(values_in):
    return lax.optimization_barrier(values_in.astype(jnp.bfloat16))

def attend(query_rows, kv_pad, kv_phrase, phone_keys, phone_values, grad_out, first_frame, slot_count, aligned, seq_len):
    frames, feat_width = query_rows.shape
    block_count = frames // BLK
    head_count = feat_width // DH
    score_scale = DH ** (-0.5)

    def product(form, left, right):
        return jnp.einsum(form, left.astype(jnp.float32), right.astype(jnp.float32), preferred_element_type=jnp.float32, precision=lax.Precision.HIGHEST)
    padded = kv_pad.reshape(block_count + 2, BLK, 2 * feat_width)
    band_rows = jnp.concatenate([padded[0:block_count], padded[1:block_count + 1], padded[2:block_count + 2]], axis=1)
    phrase_rows = kv_phrase.reshape(block_count, PHRASE_SLOTS * BLK, 2 * feat_width)
    phone_pair = jnp.concatenate([phone_keys, phone_values], axis=1)
    phone_rows = jnp.broadcast_to(phone_pair[None], (block_count, PH, 2 * feat_width))
    all_rows = jnp.concatenate([band_rows, phrase_rows, phone_rows], axis=1)
    key_count = all_rows.shape[1]
    key_heads = all_rows[:, :, :feat_width].reshape(block_count, key_count, head_count, DH)
    value_heads = all_rows[:, :, feat_width:].reshape(block_count, key_count, head_count, DH)
    row_index = jnp.arange(BLK).astype(jnp.int32)
    block_index = jnp.arange(block_count).astype(jnp.int32)
    query_pos = first_frame + block_index[:, None] * BLK + row_index[None, :]
    band_cols = jnp.arange(3 * BLK).astype(jnp.int32)
    key_pos = first_frame - BLK + block_index[:, None] * BLK + band_cols[None, :]
    distance = query_pos[:, :, None] - key_pos[:, None, :]
    band_ok = (jnp.abs(distance) <= HALF_BAND) & (key_pos[:, None, :] >= 0) & (key_pos[:, None, :] < seq_len)
    slot_index = jnp.arange(PHRASE_SLOTS * BLK).astype(jnp.int32) // BLK
    phrase_ok = jnp.broadcast_to((slot_index[None, :] < slot_count[:, None])[:, None, :], (block_count, BLK, PHRASE_SLOTS * BLK))
    phone_index = jnp.arange(PH).astype(jnp.int32)
    phone_ok = jnp.abs(phone_index[None, None, :] - aligned.reshape(block_count, BLK)[:, :, None]) <= PH_HALF
    key_mask = jnp.concatenate([band_ok, phrase_ok, phone_ok], axis=2)
    query_heads = query_rows.reshape(block_count, BLK, head_count, DH)
    scores = product('irhd,ikhd->ihrk', query_heads, key_heads) * score_scale
    scores = jnp.where(key_mask[:, None], scores, masked_score)
    row_max = lax.optimization_barrier(jnp.max(scores, axis=-1, keepdims=True))
    exp_scores = jnp.exp(scores - row_max)
    prob32 = exp_scores / lax.optimization_barrier(jnp.sum(exp_scores, axis=-1, keepdims=True))
    weights_half = round_half(prob32)
    attended = round_half(product('ihrk,ikhd->irhd', weights_half, value_heads))
    grad_heads = grad_out.reshape(block_count, BLK, head_count, DH)
    delta_row = lax.optimization_barrier(jnp.sum(grad_heads.astype(jnp.float32) * attended.astype(jnp.float32), axis=-1))
    delta_row = jnp.transpose(delta_row, (0, 2, 1))[..., None]
    d_weights = product('irhd,ikhd->ihrk', grad_heads, value_heads)
    d_scores = round_half(prob32 * (d_weights - delta_row) * score_scale)
    d_query = product('ihrk,ikhd->irhd', d_scores, key_heads).reshape(frames, feat_width)
    d_key_rows = product('ihrk,irhd->ikhd', d_scores, query_heads).reshape(block_count, key_count, feat_width)
    d_value_rows = product('ihrk,irhd->ikhd', weights_half, grad_heads).reshape(block_count, key_count, feat_width)
    d_both = jnp.concatenate([d_key_rows, d_value_rows], axis=-1)
    band_grads = d_both[:, :3 * BLK].reshape(block_count, 3, BLK, 2 * feat_width)
    pad_sum = jnp.pad(band_grads[:, 0], ((0, 2), (0, 0), (0, 0))) + jnp.pad(band_grads[:, 1], ((1, 1), (0, 0), (0, 0))) + jnp.pad(band_grads[:, 2], ((2, 0), (0, 0), (0, 0)))
    phrase_grads = d_both[:, 3 * BLK:3 * BLK + PHRASE_SLOTS * BLK].reshape(block_count, PHRASE_SLOTS, BLK, 2 * feat_width)
    phone_grads = lax.optimization_barrier(jnp.sum(d_both[:, 3 * BLK + PHRASE_SLOTS * BLK:], axis=0))
    return (attended.reshape(frames, feat_width), d_query, pad_sum, phrase_grads, phone_grads)

def reference(queries, key_vectors, value_vectors, cotangent, w_out, phoneme_keys, phoneme_values, phrase_blocks, phrase_count, alignment):
    per_dev = F_DEV // BLK
    outputs = []
    d_query_list = []
    d_key_list = []
    d_value_list = []
    d_phone_keys = []
    d_phone_values = []
    weight_sum = jnp.zeros((HD, D), jnp.float32)
    for batch_index in range(BATCH):
        query_all = queries[batch_index]
        key_value_gathered = jnp.concatenate([key_vectors[batch_index], value_vectors[batch_index]], axis=1)
        zero_rim = jnp.zeros((BLK, 2 * HD), key_value_gathered.dtype)
        kv_padded = jnp.concatenate([zero_rim, key_value_gathered, zero_rim], axis=0)
        kv_blocks = key_value_gathered.reshape(NBLK, BLK, 2 * HD)
        grad_all = jnp.dot(cotangent[batch_index], w_out.T, preferred_element_type=jnp.float32).astype(jnp.bfloat16)
        block_table = phrase_blocks[batch_index]
        counts_all = phrase_count[batch_index]
        align_all = alignment[batch_index]
        phone_k = phoneme_keys[batch_index]
        phoneme_value_rows = phoneme_values[batch_index]

        def device_step(loop_index, state_tuple):
            attended_all, d_query_all, grads_total, phone_total = state_tuple
            device = jnp.asarray(loop_index).astype(jnp.int32)
            first_frame = device * F_DEV
            first_block = device * per_dev
            query_rows = lax.dynamic_slice_in_dim(query_all, first_frame, F_DEV, 0)
            kv_pad = lax.dynamic_slice_in_dim(kv_padded, first_frame, F_DEV + 2 * BLK, 0)
            own_refs = lax.dynamic_slice_in_dim(block_table, first_block, per_dev, 0)
            kv_phrase = kv_blocks[own_refs]
            slot_count = lax.dynamic_slice_in_dim(counts_all, first_block, per_dev, 0)
            aligned = lax.dynamic_slice_in_dim(align_all, first_frame, F_DEV, 0)
            grad_rows = lax.dynamic_slice_in_dim(grad_all, first_frame, F_DEV, 0)
            attended, d_query, pad_sum, phrase_grads, phone_grads = attend(query_rows, kv_pad, kv_phrase, phone_k, phoneme_value_rows, grad_rows, first_frame, slot_count, aligned, SEQ)
            low_edge = round_half(pad_sum[0:1]).astype(jnp.float32)
            high_edge = round_half(pad_sum[per_dev + 1:]).astype(jnp.float32)
            slab = jnp.concatenate([low_edge, pad_sum[1:per_dev + 1], high_edge], axis=0)
            current = lax.dynamic_slice_in_dim(grads_total, first_block, per_dev + 2, 0)
            grads_total = lax.dynamic_update_slice_in_dim(grads_total, current + slab, first_block, 0)
            sources = (own_refs // per_dev).reshape(-1)
            local_block = (own_refs % per_dev).reshape(-1)
            device_ids = jnp.arange(N_CTX).astype(jnp.int32)
            onehot = sources[:, None] == device_ids[None, :]
            slot_sum = jnp.einsum('js,jrf->srf', onehot.astype(jnp.float32), phrase_grads.reshape(-1, BLK, 2 * HD), precision=lax.Precision.HIGHEST)
            chosen = lax.optimization_barrier(jnp.max(jnp.where(onehot, local_block[:, None], 0), axis=0))
            targets = device_ids * per_dev + chosen + 1
            grads_total = grads_total.at[targets].add(round_half(slot_sum).astype(jnp.float32))
            attended_all = lax.dynamic_update_slice_in_dim(attended_all, attended, first_frame, 0)
            d_query_all = lax.dynamic_update_slice_in_dim(d_query_all, d_query.astype(jnp.bfloat16), first_frame, 0)
            phone_total = phone_total + phone_grads
            return (attended_all, d_query_all, grads_total, phone_total)
        init_state = (jnp.zeros((SEQ, HD), queries.dtype), jnp.zeros((SEQ, HD), queries.dtype), jnp.zeros((NBLK + 2, BLK, 2 * HD), jnp.float32), jnp.zeros((PH, 2 * HD), jnp.float32))
        attended_all, d_query_all, grads_total, phone_total = lax.fori_loop(0, N_CTX, device_step, init_state)
        d_both = grads_total[1:NBLK + 1].reshape(SEQ, 2 * HD).astype(jnp.bfloat16)
        phone_half = phone_total.astype(jnp.bfloat16)
        outputs.append(jnp.dot(attended_all, w_out, preferred_element_type=jnp.float32).astype(jnp.bfloat16))
        d_query_list.append(d_query_all)
        d_key_list.append(d_both[:, :HD])
        d_value_list.append(d_both[:, HD:])
        d_phone_keys.append(phone_half[:, :HD])
        d_phone_values.append(phone_half[:, HD:])
        weight_sum = weight_sum + jnp.dot(attended_all.T, cotangent[batch_index], preferred_element_type=jnp.float32)
    d_w_out = weight_sum * (1.0 / math.sqrt(BATCH * SEQ))
    return (jnp.stack(outputs), jnp.stack(d_query_list), jnp.stack(d_key_list), jnp.stack(d_value_list), jnp.stack(d_phone_keys), jnp.stack(d_phone_values), d_w_out)
```

```python
import functools
import math

import jax
import jax.numpy as jnp
from jax import lax
from jax.experimental import pallas as pl
from jax.experimental.pallas import tpu as pltpu
from jax.sharding import PartitionSpec as P

MESH = pl.DeviceIdType.MESH
ANY = pl.BlockSpec(memory_space=pl.ANY)
VMEM = pl.BlockSpec(memory_space=pltpu.VMEM)
SMEM = pl.BlockSpec(memory_space=pltpu.SMEM)
BF16 = jnp.bfloat16
F32 = jnp.float32

DH = 128
BLK = 128
HALF_BAND = 64
SLOTS = 4
PH_HALF = 16
PH = 256
N_CTX = 16
N_DP = 4
FRAMES = 512
BLOCKS = 4
FEAT = 512
MODEL = 2048
HALF = 1024
SEQ = FRAMES * N_CTX
PHC = 16
MASKED = -1e30
LOG2E = 1.4426950408889634
LINKS = 7
BIG = 60 * 1024 * 1024

NT = (((1,), (1,)), ((), ()))
NN = (((1,), (0,)), ((), ()))
TN = (((0,), (0,)), ((), ()))


def dot(a, b, dims):
    return lax.dot_general(a, b, dims, preferred_element_type=F32)


def flip_core(c):
    return c + 1 - 2 * (c % 2)


def flip_y(c):
    return c + 2 - 4 * ((c // 2) % 2)


def partner(me, j):
    if j == 0:
        return flip_core(me)
    hop, other = 1 + (j - 1) // 2, (j - 1) % 2
    low = me % 4
    low = flip_core(low) if other else low
    return ((me // 4 + hop) % 4) * 4 + low


def sender(me, j):
    if j == 0:
        return flip_core(me)
    hop, other = 1 + (j - 1) // 2, (j - 1) % 2
    low = me % 4
    low = flip_core(low) if other else low
    return ((me // 4 + 4 - hop) % 4) * 4 + low


ORDER = (3, 4, 1, 2, 5, 6, 0)


def named_block(tbl, user, owner):
    block, found = 0, 0
    for e in range(BLOCKS * SLOTS):
        entry = tbl[user * BLOCKS + e // SLOTS, e % SLOTS]
        hit = entry // BLOCKS == owner
        block = jnp.where(hit, entry % BLOCKS, block)
        found = jnp.where(hit, 1, found)
    return block, found


def enter(peers):
    barrier = pltpu.get_barrier_semaphore()
    for device in peers:
        pl.semaphore_signal(barrier, inc=1, device_id=device, device_id_type=MESH)
    pl.semaphore_wait(barrier, len(peers))


def fetch_kernel(
    tbl, k, v, cot, w, phr, halo, grad, cot_other,
    stage, ay, cot_v, cot_o, w_v, part, send, recv, near,
):
    me, head = lax.axis_index("ctx"), lax.axis_index("head")
    across = flip_y(me)
    prev, nxt = (me + N_CTX - 1) % N_CTX, (me + 1) % N_CTX
    loads = [
        pltpu.make_async_copy(cot, cot_v, near.at[0]),
        pltpu.make_async_copy(w, w_v, near.at[1]),
    ]
    for c in loads:
        c.start()

    def remote(i, src, dst, to):
        c = pltpu.make_async_remote_copy(
            src, dst, send.at[i], recv.at[i], device_id=to, device_id_type=MESH
        )
        c.start()
        return c

    enter(
        [{"ctx": across}, {"head": 1 - head}, {"ctx": prev}, {"ctx": nxt}]
        + [{"ctx": partner(me, j)} for j in range(LINKS)]
    )
    flying = [
        remote(0, k, ay.at[0], {"ctx": across}),
        remote(1, v, ay.at[1], {"ctx": across}),
    ]
    edge = BLK - HALF_BAND
    tail = BLOCKS - 1
    for j in ORDER:
        to = partner(me, j)
        block, _ = named_block(tbl, to, me)
        stage[j, :, :FEAT] = k[block]
        stage[j, :, FEAT:] = v[block]
        flying.append(remote(7 + j, stage.at[j], phr.at[me], {"ctx": to}))
        if j == ORDER[1]:
            flying += [
                remote(3, k.at[tail, pl.ds(edge, HALF_BAND)], halo.at[0, 0], {"ctx": nxt}),
                remote(4, v.at[tail, pl.ds(edge, HALF_BAND)], halo.at[0, 1], {"ctx": nxt}),
                remote(5, k.at[0, pl.ds(0, HALF_BAND)], halo.at[1, 0], {"ctx": prev}),
                remote(6, v.at[0, pl.ds(0, HALF_BAND)], halo.at[1, 1], {"ctx": prev}),
            ]
    for c in loads:
        c.wait()
    mine = pl.ds(pl.multiple_of(head * HALF, HALF), HALF)
    theirs = pl.ds(pl.multiple_of((1 - head) * HALF, HALF), HALF)

    def first(i, _):
        rows = pl.ds(pl.multiple_of(i * BLK, BLK), BLK)
        part[rows, :] = dot(cot_v[rows, :], w_v[:, mine], NT)
        return 0

    lax.fori_loop(0, BLOCKS, first, 0)
    flying[0].wait()
    flying[1].wait()
    last = [remote(2, cot_v, cot_o, {"head": 1 - head})]
    for j in ORDER:
        to = partner(me, j)
        block, _ = named_block(tbl, to, across)
        stage[LINKS + j, :, :FEAT] = ay[0, block]
        stage[LINKS + j, :, FEAT:] = ay[1, block]
        last.append(remote(14 + j, stage.at[LINKS + j], phr.at[across], {"ctx": to}))
    block, _ = named_block(tbl, me, across)
    stage[2 * LINKS, :, :FEAT] = ay[0, block]
    stage[2 * LINKS, :, FEAT:] = ay[1, block]
    own = pltpu.make_async_copy(stage.at[2 * LINKS], phr.at[across], near.at[0])
    own.start()
    last[0].wait()
    keep = pltpu.make_async_copy(cot_o, cot_other, near.at[1])
    keep.start()

    def second(i, _):
        rows = pl.ds(pl.multiple_of(i * BLK, BLK), BLK)
        both = part[rows, :] + dot(cot_o[rows, :], w_v[:, theirs], NT)
        grad[rows, :] = both.astype(BF16)
        return 0

    lax.fori_loop(0, BLOCKS, second, 0)
    own.wait()
    keep.wait()
    for c in flying[2:] + last[1:]:
        c.wait()


def fetch(tbl, k, v, cot, w):
    return pl.pallas_call(
        fetch_kernel,
        out_shape=(
            jax.ShapeDtypeStruct((N_CTX, BLK, 2 * FEAT), BF16),
            jax.ShapeDtypeStruct((2, 2, HALF_BAND, FEAT), BF16),
            jax.ShapeDtypeStruct((FRAMES, FEAT), BF16),
            jax.ShapeDtypeStruct((FRAMES, HALF), BF16),
        ),
        in_specs=[SMEM, VMEM, VMEM, ANY, ANY],
        out_specs=(ANY, ANY, VMEM, ANY),
        scratch_shapes=[
            pltpu.VMEM((2 * LINKS + 1, BLK, 2 * FEAT), BF16),
            pltpu.VMEM((2, BLOCKS, BLK, FEAT), BF16),
            pltpu.VMEM((FRAMES, HALF), BF16),
            pltpu.VMEM((FRAMES, HALF), BF16),
            pltpu.VMEM((FEAT, MODEL), BF16),
            pltpu.VMEM((FRAMES, FEAT), F32),
            pltpu.SemaphoreType.DMA((21,)),
            pltpu.SemaphoreType.DMA((21,)),
            pltpu.SemaphoreType.DMA((2,)),
        ],
        compiler_params=pltpu.CompilerParams(
            collective_id=0, has_side_effects=True, vmem_limit_bytes=BIG
        ),
        name="fetch",
    )(tbl, k.reshape(BLOCKS, BLK, FEAT), v.reshape(BLOCKS, BLK, FEAT), cot, w)


PH_ROWS = 128
PH_SENT = 5 * PHC
PAD = HALF_BAND


def two_heads(x):
    zero = jnp.zeros((BLK, DH), x.dtype)
    top = jnp.concatenate([x[:, :DH], zero], axis=1)
    low = jnp.concatenate([zero, x[:, DH:]], axis=1)
    return jnp.concatenate([top, low], axis=0)


def attend_kernel(
    tbl, count, align, q, k, v, grad, halo, phk, phv, phr,
    att, dq, own, rims, phones, slots,
    kpad, vpad, pk, pv, ph_all, dpad, dph, acc, band_bias, ph_bias, s_buf, p_buf,
):
    me = lax.axis_index("ctx")
    first = me * FRAMES
    for pad, src, n in ((kpad, k, 0), (vpad, v, 1)):
        pad[0:PAD, :] = halo[0, n]
        pad[PAD : PAD + FRAMES, :] = src[...]
        pad[PAD + FRAMES :, :] = halo[1, n]
    for dst, src in ((pk, phk), (pv, phv)):
        ph_all[...] = jnp.zeros_like(ph_all)
        ph_all[2 * PHC : 2 * PHC + PH, :] = src[...]
        dst[...] = ph_all[pl.ds(pl.multiple_of(me * PHC, PHC), PH_ROWS), :]
    dpad[...] = jnp.zeros_like(dpad)
    dph[...] = jnp.zeros_like(dph)

    def clear(i, _):
        acc[i] = jnp.zeros((BLK, 2 * FEAT), F32)
        return 0

    lax.fori_loop(0, N_CTX, clear, 0)
    rate = DH ** (-0.5)

    def block(i, _):
        rows = pl.ds(pl.multiple_of(i * BLK, BLK), BLK)
        wide = pl.ds(pl.multiple_of(i * BLK, BLK), 2 * BLK)
        row = lax.broadcasted_iota(jnp.int32, (2 * BLK, BLK), 0)
        col = lax.broadcasted_iota(jnp.int32, (2 * BLK, BLK), 1)
        pos = first + i * BLK - PAD + row
        seen = (jnp.abs(col - row + PAD) <= HALF_BAND) & (pos >= 0) & (pos < SEQ)
        bias = jnp.where(seen, 0.0, MASKED).astype(F32)
        band_bias[...] = jnp.concatenate([bias, bias], axis=1)
        phone = me * PHC - 2 * PHC + lax.broadcasted_iota(jnp.int32, (PH_ROWS, BLK), 0)
        near = jnp.abs(phone - align[0:1, rows]) <= PH_HALF
        near = near & (phone >= 0) & (phone < PH)
        bias = jnp.where(near, 0.0, MASKED).astype(F32)
        ph_bias[...] = jnp.concatenate([bias, bias], axis=1)
        n_used = count[0, i]
        sources = [tbl[me * BLOCKS + i, p] // BLOCKS for p in range(SLOTS)]
        slot_bias = [jnp.where(p < n_used, 0.0, MASKED).astype(F32) for p in range(SLOTS)]
        for pair in range(2):
            lanes = slice(pair * 2 * DH, (pair + 1) * 2 * DH)
            vlanes = slice(FEAT + pair * 2 * DH, FEAT + (pair + 1) * 2 * DH)
            qbd = two_heads(q[rows, lanes])
            g2 = grad[rows, lanes]
            gbd = two_heads(g2)

            def keys(c, side):
                own_pad, ph_win, where = ((kpad, pk, lanes), (vpad, pv, vlanes))[side]
                if c == 0:
                    return own_pad[wide, lanes]
                if c == 3:
                    return ph_win[:, lanes]
                return jnp.concatenate(
                    [phr[sources[2 * c - 2], :, where], phr[sources[2 * c - 1], :, where]], axis=0
                )

            sizes = (2 * BLK, 2 * BLK, 2 * BLK, PH_ROWS)
            start = (0, 2 * BLK, 4 * BLK, 6 * BLK)
            top = jnp.full((1, 2 * BLK), -3e38, F32)
            for c in range(4):
                s = dot(keys(c, 0), qbd, NT) * (rate * LOG2E)
                if c == 0:
                    s = s + band_bias[...]
                elif c == 3:
                    s = s + ph_bias[...]
                else:
                    s = jnp.concatenate(
                        [s[:BLK] + slot_bias[2 * c - 2], s[BLK:] + slot_bias[2 * c - 1]], axis=0
                    )
                s_buf[start[c] : start[c] + sizes[c], :] = s
                top = jnp.maximum(top, jnp.max(s, axis=0, keepdims=True))
            total = jnp.zeros((1, 2 * BLK), F32)
            for c in range(4):
                at = slice(start[c], start[c] + sizes[c])
                e = jnp.exp2(s_buf[at, :] - top)
                s_buf[at, :] = e
                total = total + jnp.sum(e, axis=0, keepdims=True)
            inverse = 1.0 / total
            mixed = jnp.zeros((2 * BLK, 2 * DH), F32)
            for c in range(4):
                at = slice(start[c], start[c] + sizes[c])
                p = s_buf[at, :] * inverse
                s_buf[at, :] = p
                half = p.astype(BF16)
                p_buf[at, :] = half
                mixed = mixed + dot(half, keys(c, 1), TN)
            a2 = jnp.concatenate([mixed[:BLK, :DH], mixed[BLK:, DH:]], axis=1).astype(BF16)
            att[rows, lanes] = a2
            product = g2.astype(F32) * a2.astype(F32)
            delta = jnp.concatenate(
                [
                    jnp.sum(product[:, :DH].T, axis=0, keepdims=True),
                    jnp.sum(product[:, DH:].T, axis=0, keepdims=True),
                ],
                axis=1,
            )
            dq2 = jnp.zeros((2 * BLK, 2 * DH), F32)
            for c in range(4):
                at = slice(start[c], start[c] + sizes[c])
                dw = dot(keys(c, 1), gbd, NT)
                ds = (s_buf[at, :] * (dw - delta) * rate).astype(BF16)
                dq2 = dq2 + dot(ds, keys(c, 0), TN)
                dk = dot(ds, qbd, NN)
                dv = dot(p_buf[at, :], gbd, NN)
                if c == 0:
                    dpad[wide, lanes] += dk
                    dpad[wide, vlanes] += dv
                elif c == 3:
                    dph[:, lanes] += dk
                    dph[:, vlanes] += dv
                else:
                    for n in range(2):
                        part = slice(n * BLK, (n + 1) * BLK)
                        acc[sources[2 * c - 2 + n], :, lanes] += dk[part]
                        acc[sources[2 * c - 2 + n], :, vlanes] += dv[part]
            dq[rows, lanes] = jnp.concatenate([dq2[:BLK, :DH], dq2[BLK:, DH:]], axis=1).astype(BF16)
        return 0

    lax.fori_loop(0, BLOCKS, block, 0)

    def close(i, _):
        slots[i] = acc[i].astype(BF16)
        return 0

    lax.fori_loop(0, N_CTX, close, 0)
    own[...] = dpad[PAD : PAD + FRAMES, :]
    rims[0] = dpad[:PAD, :].astype(BF16)
    rims[1] = dpad[PAD + FRAMES :, :].astype(BF16)
    phones[...] = dph[:PH_SENT, :].astype(BF16)


def attend(tbl, count, align, q, k, v, grad, halo, phk, phv, phr):
    keys = 6 * BLK + PH_ROWS
    return pl.pallas_call(
        attend_kernel,
        out_shape=(
            jax.ShapeDtypeStruct((FRAMES, FEAT), BF16),
            jax.ShapeDtypeStruct((FRAMES, FEAT), BF16),
            jax.ShapeDtypeStruct((FRAMES, 2 * FEAT), F32),
            jax.ShapeDtypeStruct((2, HALF_BAND, 2 * FEAT), BF16),
            jax.ShapeDtypeStruct((PH_SENT, 2 * FEAT), BF16),
            jax.ShapeDtypeStruct((N_CTX, BLK, 2 * FEAT), BF16),
        ),
        in_specs=[SMEM, SMEM] + [VMEM] * 9,
        out_specs=(VMEM,) * 6,
        scratch_shapes=[
            pltpu.VMEM((FRAMES + 2 * PAD, FEAT), BF16),
            pltpu.VMEM((FRAMES + 2 * PAD, FEAT), BF16),
            pltpu.VMEM((PH_ROWS, FEAT), BF16),
            pltpu.VMEM((PH_ROWS, FEAT), BF16),
            pltpu.VMEM((PH + 2 * PHC + PH_ROWS, FEAT), BF16),
            pltpu.VMEM((FRAMES + 2 * PAD, 2 * FEAT), F32),
            pltpu.VMEM((PH_ROWS, 2 * FEAT), F32),
            pltpu.VMEM((N_CTX, BLK, 2 * FEAT), F32),
            pltpu.VMEM((2 * BLK, 2 * BLK), F32),
            pltpu.VMEM((PH_ROWS, 2 * BLK), F32),
            pltpu.VMEM((keys, 2 * BLK), F32),
            pltpu.VMEM((keys, 2 * BLK), BF16),
        ],
        compiler_params=pltpu.CompilerParams(vmem_limit_bytes=BIG),
        name="attend",
    )(tbl, count, align, q, k, v, grad, halo, phk, phv, phr)


SLAB = 32
CTX_SLAB = SLAB * N_DP


def giveback_kernel(
    tbl, att, own, rims, phones, slots, cot, cot_other, w,
    layer, dk, dv, dphk, dphv, dw,
    relayed, direct, relay_sum, summed, rims_in, ph_in, ph_sum, ph_all, ph_own,
    own_v, cot_v, w_v, part_out, part_in, part_own, dw_out, dw_in, dw_mid, dw_last,
    send, recv, near,
):
    me, head, lane = lax.axis_index("ctx"), lax.axis_index("head"), lax.axis_index("dp")
    across = flip_y(me)
    prev, nxt = (me + N_CTX - 1) % N_CTX, (me + 1) % N_CTX
    loads = [
        pltpu.make_async_copy(w, w_v, near.at[0]),
        pltpu.make_async_copy(cot, cot_v.at[0], near.at[1]),
        pltpu.make_async_copy(cot_other, cot_v.at[1], near.at[2]),
        pltpu.make_async_copy(own, own_v, near.at[3]),
        pltpu.make_async_copy(phones.at[pl.ds(2 * PHC, PHC)], ph_own, near.at[4]),
    ]
    for c in loads:
        c.start()

    def remote(i, src, dst, to):
        c = pltpu.make_async_remote_copy(
            src, dst, send.at[i], recv.at[i], device_id=to, device_id_type=MESH
        )
        c.start()
        return c

    enter(
        [{"head": 1 - head}]
        + [{"ctx": (me + s) % N_CTX} for s in range(1, N_CTX)]
        + [{"dp": (lane + s) % N_DP} for s in range(1, N_DP)]
    )
    to_relay, straight = {}, {}
    for j in ORDER:
        to = partner(me, j)
        to_relay[j] = remote(j, slots.at[flip_y(to)], relayed.at[j], {"ctx": to})
    rim_copies = [
        remote(18, rims.at[0], rims_in.at[0], {"ctx": prev}),
        remote(19, rims.at[1], rims_in.at[1], {"ctx": nxt}),
    ]
    ph_copies = []
    for n, (chunk, by) in enumerate(((0, -2), (1, -1), (3, 1), (4, 2))):
        to = (me + N_CTX + by) % N_CTX
        src = phones.at[pl.ds(chunk * PHC, PHC)]
        ph_copies.append(remote(24 + n, src, ph_in.at[n], {"ctx": to}))
    local = pltpu.make_async_copy(slots.at[across], relayed.at[LINKS], near.at[5])
    local.start()
    loads[0].wait()
    mine = pl.ds(pl.multiple_of(head * HALF, HALF), HALF)
    theirs = pl.ds(pl.multiple_of((1 - head) * HALF, HALF), HALF)
    out_copies = []
    for i in range(BLOCKS):
        rows = pl.ds(i * BLK, BLK)
        part_out[rows, :] = dot(att[rows, :], w_v[:, theirs], NN).astype(BF16)
        out_copies.append(
            remote(20 + i, part_out.at[rows], part_in.at[rows], {"head": 1 - head})
        )
    for j in ORDER:
        to = partner(me, j)
        straight[j] = remote(7 + j, slots.at[to], direct.at[j], {"ctx": to})
    loads[1].wait()
    loads[2].wait()
    for side, half in ((0, head), (1, 1 - head)):
        for n in range(N_CTX // 2):
            cols = slice(n * CTX_SLAB, (n + 1) * CTX_SLAB)
            piece = dot(cot_v[side, :, cols], att[...], TN).astype(BF16)
            at = pl.ds(pl.multiple_of((half * (N_CTX // 2) + n) * SLAB, SLAB), SLAB)
            for d in range(N_DP):
                dw_out[d, at, :] = piece[d * SLAB : (d + 1) * SLAB]
    dw_copies = []
    for s in range(1, N_DP):
        to = (lane + s) % N_DP
        dw_copies.append(remote(42 + s, dw_out.at[to], dw_in.at[s - 1], {"dp": to}))

    def project(i, _):
        rows = pl.ds(pl.multiple_of(i * BLK, BLK), BLK)
        part_own[rows, :] = dot(att[rows, :], w_v[:, mine], NN)
        return 0

    lax.fori_loop(0, BLOCKS, project, 0)
    loads[4].wait()
    for c in ph_copies:
        c.wait()
    total = ph_own[...].astype(F32)
    for n, by in ((0, 2), (1, 1), (2, -1), (3, -2)):
        origin = me + by
        there = (origin >= 0) & (origin < N_CTX)
        total = total + jnp.where(there, ph_in[n].astype(F32), 0.0)
    ph_sum[...] = total.astype(BF16)
    ph_all[me] = ph_sum[...]
    ph_bcast = [
        remote(27 + s, ph_sum, ph_all.at[me], {"ctx": (me + s) % N_CTX}) for s in range(1, N_CTX)
    ]
    for c in dw_copies:
        c.wait()

    def over_dp(i, _):
        rows = pl.ds(pl.multiple_of(i * SLAB, SLAB), SLAB)
        t = dw_out[lane, rows, :].astype(F32)
        for s in range(N_DP - 1):
            t = t + dw_in[s, rows, :].astype(F32)
        dw_mid[i] = t.astype(BF16)
        return 0

    lax.fori_loop(0, N_CTX, over_dp, 0)
    dw_bcast = []
    for s in range(1, N_CTX):
        to = (me + s) % N_CTX
        dw_bcast.append(remote(45 + s, dw_mid.at[to], dw_last.at[s - 1], {"ctx": to}))
    local.wait()
    for j in ORDER:
        to_relay[j].wait()
    origins = [sender(me, j) for j in range(LINKS)] + [me]
    weights = []
    for u in origins:
        block, found = named_block(tbl, u, across)
        weights.append(
            [jnp.where((block == b) & (found == 1), 1.0, 0.0).astype(F32) for b in range(BLOCKS)]
        )
    relay_copies = []
    STEP = 16
    for b in range(BLOCKS):
        def add(i, _, b=b):
            rows = pl.ds(pl.multiple_of(i * STEP, STEP), STEP)
            t = relayed[0, rows, :].astype(F32) * weights[0][b]
            for n in range(1, LINKS + 1):
                t = t + relayed[n, rows, :].astype(F32) * weights[n][b]
            relay_sum[b, rows, :] = t.astype(BF16)
            return 0

        lax.fori_loop(0, BLK // STEP, add, 0)
        relay_copies.append(remote(14 + b, relay_sum.at[b], summed.at[b], {"ctx": across}))
    for i in range(BLOCKS):
        out_copies[i].wait()
        rows = pl.ds(i * BLK, BLK)
        layer[rows, :] = (part_own[rows, :] + part_in[rows, :].astype(F32)).astype(BF16)
    for c in ph_bcast:
        c.wait()
    for i in range(N_CTX):
        at = slice(i * PHC, (i + 1) * PHC)
        dphk[at, :] = ph_all[i, :, :FEAT]
        dphv[at, :] = ph_all[i, :, FEAT:]
    for c in dw_bcast:
        c.wait()
    t = dw_mid[me].astype(F32)
    for s in range(N_CTX - 1):
        t = t + dw_last[s].astype(F32)
    dw[...] = t * (1.0 / math.sqrt(N_DP * SEQ))
    loads[3].wait()
    for c in rim_copies:
        c.wait()
    own_v[FRAMES - HALF_BAND :, :] += jnp.where(me < N_CTX - 1, rims_in[0].astype(F32), 0.0)
    own_v[:HALF_BAND, :] += jnp.where(me > 0, rims_in[1].astype(F32), 0.0)
    for j in ORDER:
        straight[j].wait()
    weights2 = []
    for u in origins[:LINKS]:
        block, found = named_block(tbl, u, me)
        weights2.append(
            [jnp.where((block == b) & (found == 1), 1.0, 0.0).astype(F32) for b in range(BLOCKS)]
        )
    for b in range(BLOCKS):
        relay_copies[b].wait()

        def finish(i, _, b=b):
            rows = pl.ds(pl.multiple_of(i * STEP, STEP), STEP)
            here = pl.ds(pl.multiple_of(b * BLK + i * STEP, STEP), STEP)
            t = own_v[here, :] + summed[b, rows, :].astype(F32)
            for n in range(LINKS):
                t = t + direct[n, rows, :].astype(F32) * weights2[n][b]
            dk[here, :] = t[:, :FEAT].astype(BF16)
            dv[here, :] = t[:, FEAT:].astype(BF16)
            return 0

        lax.fori_loop(0, BLK // STEP, finish, 0)


def giveback(tbl, att, own, rims, phones, slots, cot, cot_other, w):
    return pl.pallas_call(
        giveback_kernel,
        out_shape=(
            jax.ShapeDtypeStruct((FRAMES, HALF), BF16),
            jax.ShapeDtypeStruct((FRAMES, FEAT), BF16),
            jax.ShapeDtypeStruct((FRAMES, FEAT), BF16),
            jax.ShapeDtypeStruct((PH, FEAT), BF16),
            jax.ShapeDtypeStruct((PH, FEAT), BF16),
            jax.ShapeDtypeStruct((SLAB, FEAT), F32),
        ),
        in_specs=[SMEM, VMEM] + [ANY] * 7,
        out_specs=(VMEM,) * 6,
        scratch_shapes=[
            pltpu.VMEM((LINKS + 1, BLK, 2 * FEAT), BF16),
            pltpu.VMEM((LINKS, BLK, 2 * FEAT), BF16),
            pltpu.VMEM((BLOCKS, BLK, 2 * FEAT), BF16),
            pltpu.VMEM((BLOCKS, BLK, 2 * FEAT), BF16),
            pltpu.VMEM((2, HALF_BAND, 2 * FEAT), BF16),
            pltpu.VMEM((4, PHC, 2 * FEAT), BF16),
            pltpu.VMEM((PHC, 2 * FEAT), BF16),
            pltpu.VMEM((N_CTX, PHC, 2 * FEAT), BF16),
            pltpu.VMEM((PHC, 2 * FEAT), BF16),
            pltpu.VMEM((FRAMES, 2 * FEAT), F32),
            pltpu.VMEM((2, FRAMES, HALF), BF16),
            pltpu.VMEM((FEAT, MODEL), BF16),
            pltpu.VMEM((FRAMES, HALF), BF16),
            pltpu.VMEM((FRAMES, HALF), BF16),
            pltpu.VMEM((FRAMES, HALF), F32),
            pltpu.VMEM((N_DP, N_CTX * SLAB, FEAT), BF16),
            pltpu.VMEM((N_DP - 1, N_CTX * SLAB, FEAT), BF16),
            pltpu.VMEM((N_CTX, SLAB, FEAT), BF16),
            pltpu.VMEM((N_CTX - 1, SLAB, FEAT), BF16),
            pltpu.SemaphoreType.DMA((61,)),
            pltpu.SemaphoreType.DMA((61,)),
            pltpu.SemaphoreType.DMA((6,)),
        ],
        compiler_params=pltpu.CompilerParams(
            collective_id=1, has_side_effects=True, vmem_limit_bytes=BIG
        ),
        name="giveback",
    )(tbl, att, own, rims, phones, slots, cot, cot_other, w)


def local(q, k, v, cot, w, phk, phv, tbl, count, align):
    q, k, v, cot, phk, phv, tbl = q[0], k[0], v[0], cot[0], phk[0], phv[0], tbl[0]
    phr, halo, grad, cot_other = fetch(tbl, k, v, cot, w)
    att, dq, own, rims, phones, slots = attend(
        tbl, count, align, q, k, v, grad, halo, phk, phv, phr
    )
    layer, dk, dv, dphk, dphv, dw = giveback(
        tbl, att, own, rims, phones, slots, cot, cot_other, w
    )
    return (layer[None], dq[None], dk[None], dv[None], dphk[None], dphv[None], dw.T)


def solution(mesh):
    placed = (
        P("dp", "ctx", "head"),
        P("dp", "ctx", "head"),
        P("dp", "ctx", "head"),
        P("dp", "ctx", "head"),
        P("head", None),
        P("dp", None, "head"),
        P("dp", None, "head"),
        P("dp", None, None),
        P("dp", "ctx"),
        P("dp", "ctx"),
    )
    return jax.shard_map(
        local,
        mesh=mesh,
        in_specs=placed,
        out_specs=(
            P("dp", "ctx", "head"),
            P("dp", "ctx", "head"),
            P("dp", "ctx", "head"),
            P("dp", "ctx", "head"),
            P("dp", None, "head"),
            P("dp", None, "head"),
            P("head", ("ctx", "dp")),
        ),
        check_vma=False,
    )
```

```python
import functools
import math

import jax
import jax.numpy as jnp
from jax import lax
from jax.experimental import pallas as pl
from jax.experimental.pallas import tpu as pltpu
from jax.sharding import PartitionSpec as P

MESH = pl.DeviceIdType.MESH
ANY = pl.BlockSpec(memory_space=pl.ANY)
VMEM = pl.BlockSpec(memory_space=pltpu.VMEM)
SMEM = pl.BlockSpec(memory_space=pltpu.SMEM)
BF16 = jnp.bfloat16
F32 = jnp.float32

DH = 128
BLK = 128
HALF_BAND = 64
SLOTS = 4
PH_HALF = 16
PH = 256
N_CTX = 16
N_DP = 4
FRAMES = 512
BLOCKS = 4
FEAT = 512
MODEL = 2048
HALF = 1024
SEQ = FRAMES * N_CTX
PHC = 16
MASKED = -1e30
LOG2E = 1.4426950408889634
LINKS = 7
BIG = 60 * 1024 * 1024

NT = (((1,), (1,)), ((), ()))
NN = (((1,), (0,)), ((), ()))
TN = (((0,), (0,)), ((), ()))


def dot(a, b, dims):
    return lax.dot_general(a, b, dims, preferred_element_type=F32)


def flip_core(c):
    return c + 1 - 2 * (c % 2)


def flip_y(c):
    return c + 2 - 4 * ((c // 2) % 2)


def partner(me, j):
    if j == 0:
        return flip_core(me)
    hop, other = 1 + (j - 1) // 2, (j - 1) % 2
    low = me % 4
    low = flip_core(low) if other else low
    return ((me // 4 + hop) % 4) * 4 + low


def sender(me, j):
    if j == 0:
        return flip_core(me)
    hop, other = 1 + (j - 1) // 2, (j - 1) % 2
    low = me % 4
    low = flip_core(low) if other else low
    return ((me // 4 + 4 - hop) % 4) * 4 + low


ORDER = (3, 4, 1, 2, 5, 6, 0)


def named_block(tbl, user, owner):
    block, found = 0, 0
    for e in range(BLOCKS * SLOTS):
        entry = tbl[e % SLOTS, user * BLOCKS + e // SLOTS]
        hit = entry // BLOCKS == owner
        block = jnp.where(hit, entry % BLOCKS, block)
        found = jnp.where(hit, 1, found)
    return block, found


def enter(peers):
    barrier = pltpu.get_barrier_semaphore()
    for device in peers:
        pl.semaphore_signal(barrier, inc=1, device_id=device, device_id_type=MESH)
    pl.semaphore_wait(barrier, len(peers))


PAIRS = 2
WIDE = 2 * DH
PH_ROWS = 128
PAD = HALF_BAND
NONE = BLOCKS * SLOTS
SLAB = 32
OCT = N_CTX // 2
W_PART = FEAT // (2 * N_DP)
STEP = 16
KEYS = 6 * BLK + PH_ROWS

S_W, S_WG, S_AY, S_P, S_HALO, S_OWN, S_FWD = 0, 1, 8, 12, 13, 17, 31
S_R, S_D, S_Y, S_ATT, S_RIM, S_PHC, S_PHB, S_PHX = 45, 59, 73, 81, 83, 85, 89, 96
S_DWC, S_DWX, S_DWT, S_DWL, S_ALL = 97, 98, 101, 108, 109


def two_heads(x):
    zero = jnp.zeros((BLK, DH), x.dtype)
    top = jnp.concatenate([x[:, :DH], zero], axis=1)
    low = jnp.concatenate([zero, x[:, DH:]], axis=1)
    return jnp.concatenate([top, low], axis=0)


def layer_kernel(
    tbl, count, align, k, v, q, cot, w, phk, phv,
    layer, dq, dk, dv, dphk, dphv, dw,
    stage, ay0, ay1, phr0, phr1, cot_v, w_m, w_o, part, p_out, p_in, grad, q_v, kpad, vpad, pk, pv, ph_tmp,
    dpad, dph, run, g, s_buf, p_buf, band_bias, ph_bias, relayed, direct, rsum, summed,
    rims, rims_in, ph_out, ph_in, ph_mine, ph_all, att, att_o,
    dwx, dwc, dws, dwr, dwm, dwl, dwe, dwf, send, recv, near,
):
    ay, phr = (ay0, ay1), (phr0, phr1)
    me, head, lane = lax.axis_index("ctx"), lax.axis_index("head"), lax.axis_index("dp")
    across, twin = flip_y(me), flip_core(me)
    prev, nxt = (me + N_CTX - 1) % N_CTX, (me + 1) % N_CTX
    parity = me % 2
    first = me * FRAMES
    mine = pl.ds(pl.multiple_of(head * HALF, HALF), HALF)
    theirs = pl.ds(pl.multiple_of((1 - head) * HALF, HALF), HALF)
    loads = [
        pltpu.make_async_copy(cot, cot_v, near.at[0]),
        pltpu.make_async_copy(w.at[:, mine], w_m, near.at[1]),
        pltpu.make_async_copy(q, q_v, near.at[2]),
    ]
    for c in loads:
        c.start()

    def remote(i, src, dst, **to):
        c = pltpu.make_async_remote_copy(
            src, dst, send.at[i], recv.at[i], device_id=to, device_id_type=MESH
        )
        c.start()
        return c

    mesh_peers = [{"ctx": (me + s) % N_CTX} for s in range(1, N_CTX)]
    mesh_peers += [{"dp": (lane + s) % N_DP} for s in range(1, N_DP)]
    mesh_peers += [{"ctx": twin, "dp": (lane + s) % N_DP} for s in range(1, N_DP)]
    mesh_peers += [{"head": 1 - head}, {"ctx": (me + OCT) % N_CTX, "head": 1 - head}]
    enter(mesh_peers)

    eighth = pl.ds(pl.multiple_of((lane * 2 + parity) * W_PART, W_PART), W_PART)
    w_first = remote(S_W, w.at[eighth, theirs], w_o.at[eighth], head=1 - head)

    def across_copies(p):
        lanes = pl.ds(p * WIDE, WIDE)
        return [
            remote(S_AY + 2 * p + n, src.at[:, :, lanes], ay[p].at[n], ctx=across)
            for n, src in enumerate((k, v))
        ]

    ay_copies = [across_copies(0)]
    kv_copies = [[], []]
    own_block = {j: named_block(tbl, partner(me, j), me)[0] for j in ORDER}

    def send_own(p):
        for j in ORDER:
            lanes = slice(p * WIDE, (p + 1) * WIDE)
            stage[p, j, :, :WIDE] = k[own_block[j], :, lanes]
            stage[p, j, :, WIDE:] = v[own_block[j], :, lanes]
            kv_copies[p].append(
                remote(S_OWN + LINKS * p + j, stage.at[p, j], phr[p].at[me], ctx=partner(me, j))
            )

    far_block = {}

    def send_far(p):
        for j in ORDER:
            stage[p, LINKS + j, :, :WIDE] = ay[p][0, far_block[j]]
            stage[p, LINKS + j, :, WIDE:] = ay[p][1, far_block[j]]
            kv_copies[p].append(
                remote(
                    S_FWD + LINKS * p + j, stage.at[p, LINKS + j], phr[p].at[across],
                    ctx=partner(me, j),
                )
            )
        phr[p][across, :, :WIDE] = ay[p][0, far_block[LINKS]]
        phr[p][across, :, WIDE:] = ay[p][1, far_block[LINKS]]

    send_own(0)
    tail = pl.ds(BLK - PAD, PAD)
    halo_copies = []
    for n, (src, dst) in enumerate(((k, kpad), (v, vpad))):
        halo_copies += [
            remote(S_HALO + n, src.at[BLOCKS - 1, tail], dst.at[pl.ds(0, PAD)], ctx=nxt),
            remote(
                S_HALO + 2 + n, src.at[0, pl.ds(0, PAD)], dst.at[pl.ds(PAD + FRAMES, PAD)],
                ctx=prev,
            ),
        ]
    for j in ORDER:
        far_block[j] = named_block(tbl, partner(me, j), across)[0]
    far_block[LINKS] = named_block(tbl, me, across)[0]
    w_first.wait()
    w_copies = []
    for n in range(LINKS):
        hop, other = (n + 1) // 2, (n + 1) % 2
        w_copies.append(
            remote(
                S_WG + n, w_o.at[eighth], w_o.at[eighth],
                ctx=twin if other else me, dp=(lane + hop) % N_DP,
            )
        )
    for pad, src in ((kpad, k), (vpad, v)):
        for b in range(BLOCKS):
            pad[PAD + b * BLK : PAD + (b + 1) * BLK, :] = src[b]
    for dst, src in ((pk, phk), (pv, phv)):
        ph_tmp[...] = jnp.zeros_like(ph_tmp)
        ph_tmp[2 * PHC : 2 * PHC + PH, :] = src[...]
        dst[...] = ph_tmp[pl.ds(pl.multiple_of(me * PHC, PHC), PH_ROWS), :]
    dpad[...] = jnp.zeros_like(dpad)
    dph[...] = jnp.zeros_like(dph)
    run[NONE] = jnp.zeros((BLK, 2 * WIDE), F32)
    for c in loads:
        c.wait()

    def each_block(body):
        def step(i, _):
            body(pl.ds(pl.multiple_of(i * BLK, BLK), BLK))
            return 0

        lax.fori_loop(0, BLOCKS, step, 0)

    def own_part(rows):
        part[rows, :] = dot(cot_v[rows, :], w_m[...], NT)

    each_block(own_part)
    for c in ay_copies[0]:
        c.wait()
    ay_copies.append(across_copies(1))
    send_far(0)
    send_own(1)
    for c in w_copies:
        c.wait()

    def other_part(rows):
        p_out[rows, :] = dot(cot_v[rows, :], w_o[...], NT).astype(BF16)

    each_block(other_part)
    p_copy = remote(S_P, p_out, p_in, head=1 - head)
    for c in ay_copies[1]:
        c.wait()
    send_far(1)
    p_copy.wait()

    def whole_grad(rows):
        grad[rows, :] = (part[rows, :] + p_in[rows, :].astype(F32)).astype(BF16)

    each_block(whole_grad)
    for c in halo_copies:
        c.wait()

    rate = DH ** (-0.5)
    sources = [tbl[e % SLOTS, me * BLOCKS + e // SLOTS] // BLOCKS for e in range(NONE)]

    def attend(p):
        lanes = slice(p * WIDE, (p + 1) * WIDE)
        klanes = slice(p * 2 * WIDE, p * 2 * WIDE + WIDE)
        vlanes = slice(p * 2 * WIDE + WIDE, (p + 1) * 2 * WIDE)

        def block(i, _):
            rows = pl.ds(pl.multiple_of(i * BLK, BLK), BLK)
            wide = pl.ds(pl.multiple_of(i * BLK, BLK), 2 * BLK)
            row = lax.broadcasted_iota(jnp.int32, (2 * BLK, BLK), 0)
            col = lax.broadcasted_iota(jnp.int32, (2 * BLK, BLK), 1)
            pos = first + i * BLK - PAD + row
            seen = (jnp.abs(col - row + PAD) <= HALF_BAND) & (pos >= 0) & (pos < SEQ)
            bias = jnp.where(seen, 0.0, MASKED).astype(F32)
            band_bias[...] = jnp.concatenate([bias, bias], axis=1)
            phone = me * PHC - 2 * PHC + lax.broadcasted_iota(jnp.int32, (PH_ROWS, BLK), 0)
            near_by = jnp.abs(phone - align[0:1, rows]) <= PH_HALF
            near_by = near_by & (phone >= 0) & (phone < PH)
            bias = jnp.where(near_by, 0.0, MASKED).astype(F32)
            ph_bias[...] = jnp.concatenate([bias, bias], axis=1)
            n_used = count[0, i]
            named = [tbl[n, me * BLOCKS + i] // BLOCKS for n in range(SLOTS)]
            slot_bias = [jnp.where(n < n_used, 0.0, MASKED).astype(F32) for n in range(SLOTS)]
            qbd = two_heads(q_v[rows, lanes])
            g2 = grad[rows, lanes]
            gbd = two_heads(g2)

            def keys(c, side):
                own_pad, ph_win = ((kpad, pk), (vpad, pv))[side]
                where = slice(side * WIDE, (side + 1) * WIDE)
                if c == 0:
                    return own_pad[wide, lanes]
                if c == 3:
                    return ph_win[:, lanes]
                return jnp.concatenate(
                    [phr[p][named[2 * c - 2], :, where], phr[p][named[2 * c - 1], :, where]], axis=0
                )

            sizes = (2 * BLK, 2 * BLK, 2 * BLK, PH_ROWS)
            start = (0, 2 * BLK, 4 * BLK, 6 * BLK)
            top = jnp.full((1, 2 * BLK), -3e38, F32)
            for c in range(4):
                s = dot(keys(c, 0), qbd, NT) * (rate * LOG2E)
                if c == 0:
                    s = s + band_bias[...]
                elif c == 3:
                    s = s + ph_bias[...]
                else:
                    s = jnp.concatenate(
                        [s[:BLK] + slot_bias[2 * c - 2], s[BLK:] + slot_bias[2 * c - 1]], axis=0
                    )
                s_buf[start[c] : start[c] + sizes[c], :] = s
                top = jnp.maximum(top, jnp.max(s, axis=0, keepdims=True))
            total = jnp.zeros((1, 2 * BLK), F32)
            for c in range(4):
                at = slice(start[c], start[c] + sizes[c])
                e = jnp.exp2(s_buf[at, :] - top)
                s_buf[at, :] = e
                total = total + jnp.sum(e, axis=0, keepdims=True)
            inverse = 1.0 / total
            mixed = jnp.zeros((2 * BLK, WIDE), F32)
            for c in range(4):
                at = slice(start[c], start[c] + sizes[c])
                prob = s_buf[at, :] * inverse
                s_buf[at, :] = prob
                half = prob.astype(BF16)
                p_buf[at, :] = half
                mixed = mixed + dot(half, keys(c, 1), TN)
            a2 = jnp.concatenate([mixed[:BLK, :DH], mixed[BLK:, DH:]], axis=1).astype(BF16)
            att[rows, lanes] = a2
            product = g2.astype(F32) * a2.astype(F32)
            delta = jnp.concatenate(
                [
                    jnp.sum(product[:, :DH].T, axis=0, keepdims=True),
                    jnp.sum(product[:, DH:].T, axis=0, keepdims=True),
                ],
                axis=1,
            )
            dq2 = jnp.zeros((2 * BLK, WIDE), F32)
            for c in range(4):
                at = slice(start[c], start[c] + sizes[c])
                d_weight = dot(keys(c, 1), gbd, NT)
                ds = (s_buf[at, :] * (d_weight - delta) * rate).astype(BF16)
                dq2 = dq2 + dot(ds, keys(c, 0), TN)
                dk2 = dot(ds, qbd, NN)
                dv2 = dot(p_buf[at, :], gbd, NN)
                if c == 0:
                    dpad[wide, klanes] += dk2
                    dpad[wide, vlanes] += dv2
                elif c == 3:
                    dph[:, klanes] += dk2
                    dph[:, vlanes] += dv2
                else:
                    for n in range(2):
                        slot = 2 * c - 2 + n
                        here = i * SLOTS + slot
                        before = NONE
                        for e in range(NONE):
                            same = (sources[e] == named[slot]) & (here > e)
                            before = jnp.where(same, e, before)
                        half_rows = slice(n * BLK, (n + 1) * BLK)
                        run[here, :, :WIDE] = dk2[half_rows] + run[before, :, :WIDE]
                        run[here, :, WIDE:] = dv2[half_rows] + run[before, :, WIDE:]
            dq[rows, lanes] = jnp.concatenate([dq2[:BLK, :DH], dq2[BLK:, DH:]], axis=1).astype(BF16)
            return 0

        lax.fori_loop(0, BLOCKS, block, 0)

    def grads_of(owner):
        last = NONE
        for e in range(NONE):
            last = jnp.where(sources[e] == owner, e, last)
        return run[last].astype(BF16)

    to_relay, straight, att_copies = [{}, {}], [{}, {}], []

    def collect(p):
        for j in ORDER:
            to = partner(me, j)
            g[p, j] = grads_of(flip_y(to))
            to_relay[p][j] = remote(
                S_R + LINKS * p + j, g.at[p, j], relayed.at[p, j], ctx=to
            )
        lanes = pl.ds(p * WIDE, WIDE)
        att_copies.append(
            remote(S_ATT + p, att.at[:, lanes], att_o.at[:, lanes], head=1 - head)
        )
        relayed[p, LINKS] = grads_of(across)
        for j in ORDER:
            g[p, LINKS + j] = grads_of(partner(me, j))

    def send_straight(p):
        for j in ORDER:
            straight[p][j] = remote(
                S_D + LINKS * p + j, g.at[p, LINKS + j], direct.at[p, j], ctx=partner(me, j)
            )

    for c in kv_copies[0]:
        c.wait()
    attend(0)
    collect(0)
    for c in kv_copies[1]:
        c.wait()
    attend(1)
    collect(1)
    send_straight(0)
    rims[0] = dpad[:PAD, :].astype(BF16)
    rims[1] = dpad[PAD + FRAMES :, :].astype(BF16)
    rim_copies = [
        remote(S_RIM, rims.at[0], rims_in.at[0], ctx=prev),
        remote(S_RIM + 1, rims.at[1], rims_in.at[1], ctx=nxt),
    ]
    ph_copies = []
    for n, (chunk, by) in enumerate(((0, -2), (1, -1), (3, 1), (4, 2))):
        ph_out[n] = dph[chunk * PHC : (chunk + 1) * PHC, :].astype(BF16)
        ph_copies.append(remote(S_PHC + n, ph_out.at[n], ph_in.at[n], ctx=(me + N_CTX + by) % N_CTX))

    def slabs(features, side):
        def step(n, _):
            cols = pl.ds(pl.multiple_of(n * BLK, BLK), BLK)
            piece = dot(cot_v[:, cols], features[...], TN).astype(BF16)
            at = side * (OCT // 2) + n // 2
            for d in range(N_DP):
                dwx[n % 2, d, at] = piece[d * SLAB : (d + 1) * SLAB]
            return 0

        lax.fori_loop(0, OCT, step, 0)

    slabs(att, head)
    weights_far, weights_own = [], []
    for u in [sender(me, j) for j in range(LINKS)] + [me]:
        for owner, weights in ((across, weights_far), (me, weights_own)):
            block, found = named_block(tbl, u, owner)
            weights.append(
                [jnp.where((block == b) & (found == 1), 1.0, 0.0).astype(F32) for b in range(BLOCKS)]
            )
    relay_copies = [[], []]

    def relay(p):
        for j in ORDER:
            to_relay[p][j].wait()
        for b in range(BLOCKS):

            def add(i, _, b=b):
                rows = pl.ds(pl.multiple_of(i * STEP, STEP), STEP)
                t = relayed[p, 0, rows, :].astype(F32) * weights_far[0][b]
                for n in range(1, LINKS + 1):
                    t = t + relayed[p, n, rows, :].astype(F32) * weights_far[n][b]
                rsum[p, b, rows, :] = t.astype(BF16)
                return 0

            lax.fori_loop(0, BLK // STEP, add, 0)
            relay_copies[p].append(
                remote(S_Y + BLOCKS * p + b, rsum.at[p, b], summed.at[p, b], ctx=across)
            )

    relay(0)
    send_straight(1)
    for c in att_copies:
        c.wait()
    slabs(att_o, 1 - head)
    dw_core = remote(S_DWC, dwx.at[1 - parity], dwc, ctx=twin)

    def project(rows):
        t = dot(att[rows, :], w_m[...], NN) + dot(att_o[rows, :], w_o[...], NN)
        layer[rows, :] = t.astype(BF16)

    each_block(project)
    for c in ph_copies:
        c.wait()
    total = dph[2 * PHC : 3 * PHC, :]
    for n, by in ((0, 2), (1, 1), (2, -1), (3, -2)):
        origin = me + by
        there = (origin >= 0) & (origin < N_CTX)
        total = total + jnp.where(there, ph_in[n].astype(F32), 0.0)
    ph_mine[...] = total.astype(BF16)
    ph_all[parity, me // 2] = ph_mine[...]
    ph_bcast = [
        remote(S_PHB + s - 1, ph_mine, ph_all.at[parity, me // 2], ctx=(me + 2 * s) % N_CTX)
        for s in range(1, OCT)
    ]
    dw_core.wait()

    def over_core(i, _):
        for d in range(N_DP):
            dws[d, i] = (dwx[parity, d, i].astype(F32) + dwc[d, i].astype(F32)).astype(BF16)
        return 0

    lax.fori_loop(0, OCT, over_core, 0)
    dw_x = [
        remote(S_DWX + s - 1, dws.at[(lane + s) % N_DP], dwr.at[s - 1], dp=(lane + s) % N_DP)
        for s in range(1, N_DP)
    ]
    for c in ph_bcast:
        c.wait()
    ph_core = remote(S_PHX, ph_all.at[parity], ph_all.at[parity], ctx=twin)
    relay(1)
    for c in dw_x:
        c.wait()

    def over_dp(i, _):
        t = dws[lane, i].astype(F32)
        for s in range(N_DP - 1):
            t = t + dwr[s, i].astype(F32)
        dwm[i] = t.astype(BF16)
        return 0

    lax.fori_loop(0, OCT, over_dp, 0)
    dw_t = []
    for s in range(1, OCT):
        to = (me + 2 * s) % N_CTX
        dw_t.append(remote(S_DWT + s - 1, dwm.at[to // 2], dwl.at[s - 1], ctx=to))

    def finish(p):
        for j in ORDER:
            straight[p][j].wait()
        lanes = slice(p * WIDE, (p + 1) * WIDE)
        both = slice(p * 2 * WIDE, (p + 1) * 2 * WIDE)
        for b in range(BLOCKS):
            relay_copies[p][b].wait()

            def add(i, _, b=b):
                rows = pl.ds(pl.multiple_of(i * STEP, STEP), STEP)
                here = pl.ds(pl.multiple_of(b * BLK + i * STEP, STEP), STEP)
                there = pl.ds(pl.multiple_of(PAD + b * BLK + i * STEP, STEP), STEP)
                t = dpad[there, both] + summed[p, b, rows, :].astype(F32)
                for n in range(LINKS):
                    t = t + direct[p, n, rows, :].astype(F32) * weights_own[n][b]
                dk[here, lanes] = t[:, :WIDE].astype(BF16)
                dv[here, lanes] = t[:, WIDE:].astype(BF16)
                return 0

            lax.fori_loop(0, BLK // STEP, add, 0)

    for c in rim_copies:
        c.wait()
    low, high = slice(PAD, 2 * PAD), slice(FRAMES, FRAMES + PAD)
    dpad[high, :] += jnp.where(me < N_CTX - 1, rims_in[0].astype(F32), 0.0)
    dpad[low, :] += jnp.where(me > 0, rims_in[1].astype(F32), 0.0)
    finish(0)
    for c in dw_t:
        c.wait()
    t = dwm[me // 2].astype(F32)
    for s in range(OCT - 1):
        t = t + dwl[s].astype(F32)
    dwe[...] = t * (1.0 / math.sqrt(N_DP * SEQ))
    dw_last = remote(S_DWL, dwe, dwf, ctx=(me + OCT) % N_CTX, head=1 - head)
    ph_core.wait()
    for i in range(N_CTX):
        at = slice(i * PHC, (i + 1) * PHC)
        for p in range(PAIRS):
            lanes = slice(p * WIDE, (p + 1) * WIDE)
            here = p * 2 * WIDE
            dphk[at, lanes] = ph_all[i % 2, i // 2, :, here : here + WIDE]
            dphv[at, lanes] = ph_all[i % 2, i // 2, :, here + WIDE : here + 2 * WIDE]
    dw_last.wait()
    dw[...] = jnp.where(me // OCT == head, dwe[...], dwf[...])
    finish(1)


def layer_call(tbl, count, align, k, v, q, cot, w, phk, phv):
    scratch = (
        ((PAIRS, 2 * LINKS, BLK, 2 * WIDE), BF16),
        ((2, BLOCKS, BLK, WIDE), BF16),
        ((2, BLOCKS, BLK, WIDE), BF16),
        ((N_CTX, BLK, 2 * WIDE), BF16),
        ((N_CTX, BLK, 2 * WIDE), BF16),
        ((FRAMES, HALF), BF16),
        ((FEAT, HALF), BF16),
        ((FEAT, HALF), BF16),
        ((FRAMES, FEAT), F32),
        ((FRAMES, FEAT), BF16),
        ((FRAMES, FEAT), BF16),
        ((FRAMES, FEAT), BF16),
        ((FRAMES, FEAT), BF16),
        ((FRAMES + 2 * PAD, FEAT), BF16),
        ((FRAMES + 2 * PAD, FEAT), BF16),
        ((PH_ROWS, FEAT), BF16),
        ((PH_ROWS, FEAT), BF16),
        ((PH + 2 * PHC + PH_ROWS, FEAT), BF16),
        ((FRAMES + 2 * PAD, 2 * FEAT), F32),
        ((PH_ROWS, 2 * FEAT), F32),
        ((NONE + 1, BLK, 2 * WIDE), F32),
        ((PAIRS, 2 * LINKS, BLK, 2 * WIDE), BF16),
        ((KEYS, 2 * BLK), F32),
        ((KEYS, 2 * BLK), BF16),
        ((2 * BLK, 2 * BLK), F32),
        ((PH_ROWS, 2 * BLK), F32),
        ((PAIRS, LINKS + 1, BLK, 2 * WIDE), BF16),
        ((PAIRS, LINKS, BLK, 2 * WIDE), BF16),
        ((PAIRS, BLOCKS, BLK, 2 * WIDE), BF16),
        ((PAIRS, BLOCKS, BLK, 2 * WIDE), BF16),
        ((2, PAD, 2 * FEAT), BF16),
        ((2, PAD, 2 * FEAT), BF16),
        ((4, PHC, 2 * FEAT), BF16),
        ((4, PHC, 2 * FEAT), BF16),
        ((PHC, 2 * FEAT), BF16),
        ((2, OCT, PHC, 2 * FEAT), BF16),
        ((FRAMES, FEAT), BF16),
        ((FRAMES, FEAT), BF16),
        ((2, N_DP, OCT, SLAB, FEAT), BF16),
        ((N_DP, OCT, SLAB, FEAT), BF16),
        ((N_DP, OCT, SLAB, FEAT), BF16),
        ((N_DP - 1, OCT, SLAB, FEAT), BF16),
        ((OCT, SLAB, FEAT), BF16),
        ((OCT - 1, SLAB, FEAT), BF16),
        ((SLAB, FEAT), F32),
        ((SLAB, FEAT), F32),
    )
    return pl.pallas_call(
        layer_kernel,
        out_shape=(
            jax.ShapeDtypeStruct((FRAMES, HALF), BF16),
            jax.ShapeDtypeStruct((FRAMES, FEAT), BF16),
            jax.ShapeDtypeStruct((FRAMES, FEAT), BF16),
            jax.ShapeDtypeStruct((FRAMES, FEAT), BF16),
            jax.ShapeDtypeStruct((PH, FEAT), BF16),
            jax.ShapeDtypeStruct((PH, FEAT), BF16),
            jax.ShapeDtypeStruct((SLAB, FEAT), F32),
        ),
        in_specs=[SMEM, SMEM, VMEM, VMEM, VMEM, ANY, ANY, ANY, VMEM, VMEM],
        out_specs=(VMEM,) * 7,
        scratch_shapes=[pltpu.VMEM(shape, kind) for shape, kind in scratch]
        + [
            pltpu.SemaphoreType.DMA((S_ALL,)),
            pltpu.SemaphoreType.DMA((S_ALL,)),
            pltpu.SemaphoreType.DMA((3,)),
        ],
        compiler_params=pltpu.CompilerParams(
            collective_id=0, has_side_effects=True, vmem_limit_bytes=BIG
        ),
        name="layer",
    )(
        tbl, count, align, k.reshape(BLOCKS, BLK, FEAT), v.reshape(BLOCKS, BLK, FEAT),
        q, cot, w, phk, phv,
    )


def hand_on_kernel(*refs):
    n = (len(refs) - 1) // 2
    copies = [pltpu.make_async_copy(refs[i], refs[n + i], refs[-1].at[i]) for i in range(n)]
    for c in copies:
        c.start()
    for c in copies:
        c.wait()


def hand_on(*arrays):
    n = len(arrays)
    return pl.pallas_call(
        hand_on_kernel,
        out_shape=tuple(jax.ShapeDtypeStruct(a.shape, a.dtype) for a in arrays),
        in_specs=[ANY] * n,
        out_specs=(ANY,) * n,
        scratch_shapes=[pltpu.SemaphoreType.DMA((n,))],
        name="hand_on",
    )(*arrays)


def local(q, k, v, cot, w, phk, phv, tbl, count, align):
    q, k, v, cot, phk, phv, tbl = q[0], k[0], v[0], cot[0], phk[0], phv[0], tbl[0].T
    layer, dq, dk, dv, dphk, dphv, dw = layer_call(
        tbl, count, align, k, v, q, cot, w, phk, phv
    )
    layer, dq, dk, dv, dphk, dphv, dw = hand_on(layer, dq, dk, dv, dphk, dphv, dw)
    return (layer[None], dq[None], dk[None], dv[None], dphk[None], dphv[None], dw.T)


def solution(mesh):
    placed = (
        P("dp", "ctx", "head"),
        P("dp", "ctx", "head"),
        P("dp", "ctx", "head"),
        P("dp", "ctx", "head"),
        P("head", None),
        P("dp", None, "head"),
        P("dp", None, "head"),
        P("dp", None, None),
        P("dp", "ctx"),
        P("dp", "ctx"),
    )
    return jax.shard_map(
        local,
        mesh=mesh,
        in_specs=placed,
        out_specs=(
            P("dp", "ctx", "head"),
            P("dp", "ctx", "head"),
            P("dp", "ctx", "head"),
            P("dp", "ctx", "head"),
            P("dp", None, "head"),
            P("dp", None, "head"),
            P("head", ("ctx", "dp")),
        ),
        check_vma=False,
    )
```

```python
import functools
import math

import jax
import jax.numpy as jnp
from jax import lax
from jax.experimental import pallas as pl
from jax.experimental.pallas import tpu as pltpu
from jax.sharding import PartitionSpec as P

MESH = pl.DeviceIdType.MESH
ANY = pl.BlockSpec(memory_space=pl.ANY)
VMEM = pl.BlockSpec(memory_space=pltpu.VMEM)
SMEM = pl.BlockSpec(memory_space=pltpu.SMEM)
BF16 = jnp.bfloat16
F32 = jnp.float32

DH = 128
BLK = 128
HALF_BAND = 64
SLOTS = 4
PH_HALF = 16
PH = 256
N_CTX = 16
N_DP = 4
FRAMES = 512
BLOCKS = 4
FEAT = 512
MODEL = 2048
HALF = 1024
SEQ = FRAMES * N_CTX
PHC = 16
MASKED = -1e30
LOG2E = 1.4426950408889634
LINKS = 7
BIG = 60 * 1024 * 1024

NT = (((1,), (1,)), ((), ()))
NN = (((1,), (0,)), ((), ()))
TN = (((0,), (0,)), ((), ()))


def dot(a, b, dims):
    return lax.dot_general(a, b, dims, preferred_element_type=F32)


def flip_core(c):
    return c + 1 - 2 * (c % 2)


def flip_y(c):
    return c + 2 - 4 * ((c // 2) % 2)


def partner(me, j):
    if j == 0:
        return flip_core(me)
    hop, other = 1 + (j - 1) // 2, (j - 1) % 2
    low = me % 4
    low = flip_core(low) if other else low
    return ((me // 4 + hop) % 4) * 4 + low


def sender(me, j):
    if j == 0:
        return flip_core(me)
    hop, other = 1 + (j - 1) // 2, (j - 1) % 2
    low = me % 4
    low = flip_core(low) if other else low
    return ((me // 4 + 4 - hop) % 4) * 4 + low


ORDER = (3, 4, 1, 2, 5, 6, 0)


def named_block(tbl, user, owner):
    block, found = 0, 0
    for e in range(BLOCKS * SLOTS):
        entry = tbl[e % SLOTS, user * BLOCKS + e // SLOTS]
        hit = entry // BLOCKS == owner
        block = jnp.where(hit, entry % BLOCKS, block)
        found = jnp.where(hit, 1, found)
    return block, found


PAIRS = 2
WIDE = 2 * DH
PH_ROWS = 128
PAD = HALF_BAND
NONE = BLOCKS * SLOTS
SLAB = 32
OCT = N_CTX // 2
W_PART = FEAT // (2 * N_DP)
STEP = 16
EARLY = 3
KEYS = 6 * BLK + PH_ROWS

S_W, S_WG, S_AY, S_P, S_HALO, S_OWN, S_FWD = 0, 1, 8, 12, 13, 17, 31
S_R, S_D, S_Y, S_ATT, S_RIM, S_PHC, S_PHB, S_PHX = 45, 59, 73, 81, 83, 85, 89, 96
S_DWC, S_DWX, S_DWT, S_DWL, S_ALL = 97, 98, 101, 108, 109


def two_heads(x):
    zero = jnp.zeros((BLK, DH), x.dtype)
    top = jnp.concatenate([x[:, :DH], zero], axis=1)
    low = jnp.concatenate([zero, x[:, DH:]], axis=1)
    return jnp.concatenate([top, low], axis=0)


def layer_kernel(
    tbl, count, align, k_far, v_far, q, cot, w, phk, phv,
    layer, dq, dk, dv, dphk, dphv, dw,
    k, v, stage, ay0, ay1, phr0, phr1, cot_v, w_m, w_o, part, p_out, p_in, grad, q_v, kpad, vpad, pk, pv, ph_tmp,
    dpad, dph, run, g, s_buf, p_buf, band_bias, ph_bias, relayed, direct, rsum, summed,
    rims, rims_in, ph_out, ph_in, ph_mine, ph_all, att, att_o,
    dwx, dwc, dws, dwr, dwm, dwl, dwe, dwf, send, recv, near,
):
    ay, phr = (ay0, ay1), (phr0, phr1)
    me, head, lane = lax.axis_index("ctx"), lax.axis_index("head"), lax.axis_index("dp")
    across, twin = flip_y(me), flip_core(me)
    prev, nxt = (me + N_CTX - 1) % N_CTX, (me + 1) % N_CTX
    parity = me % 2
    first = me * FRAMES
    mine = pl.ds(pl.multiple_of(head * HALF, HALF), HALF)
    theirs = pl.ds(pl.multiple_of((1 - head) * HALF, HALF), HALF)
    loads = [
        pltpu.make_async_copy(cot, cot_v, near.at[0]),
        pltpu.make_async_copy(w.at[:, mine], w_m, near.at[1]),
        pltpu.make_async_copy(q, q_v, near.at[2]),
    ]
    kv_loads = [
        pltpu.make_async_copy(k_far, k, near.at[3]),
        pltpu.make_async_copy(v_far, v, near.at[4]),
    ]
    for c in kv_loads + loads:
        c.start()

    def remote(i, src, dst, **to):
        c = pltpu.make_async_remote_copy(
            src, dst, send.at[i], recv.at[i], device_id=to, device_id_type=MESH
        )
        c.start()
        return c

    mesh_peers = [{"ctx": (me + s) % N_CTX} for s in range(1, N_CTX)]
    mesh_peers += [{"dp": (lane + s) % N_DP} for s in range(1, N_DP)]
    mesh_peers += [{"ctx": twin, "dp": (lane + s) % N_DP} for s in range(1, N_DP)]
    mesh_peers += [{"head": 1 - head}, {"ctx": (me + OCT) % N_CTX, "head": 1 - head}]
    barrier = pltpu.get_barrier_semaphore()
    for device in mesh_peers:
        pl.semaphore_signal(barrier, inc=1, device_id=device, device_id_type=MESH)
    own_block = {j: named_block(tbl, partner(me, j), me)[0] for j in ORDER}
    far_block = {j: named_block(tbl, partner(me, j), across)[0] for j in ORDER}
    far_block[LINKS] = named_block(tbl, me, across)[0]
    pl.semaphore_wait(barrier, len(mesh_peers))

    eighth = pl.ds(pl.multiple_of((lane * 2 + parity) * W_PART, W_PART), W_PART)
    w_first = remote(S_W, w.at[eighth, theirs], w_o.at[eighth], head=1 - head)

    def across_copies(p):
        lanes = pl.ds(p * WIDE, WIDE)
        return [
            remote(S_AY + 2 * p + n, src.at[:, :, lanes], ay[p].at[n], ctx=across)
            for n, src in enumerate((k_far, v_far))
        ]

    ay_copies = [across_copies(0)]
    kv_copies = [[], []]

    def send_own(p, these=ORDER):
        for j in these:
            lanes = slice(p * WIDE, (p + 1) * WIDE)
            stage[p, j, :, :WIDE] = k[own_block[j], :, lanes]
            stage[p, j, :, WIDE:] = v[own_block[j], :, lanes]
            kv_copies[p].append(
                remote(S_OWN + LINKS * p + j, stage.at[p, j], phr[p].at[me], ctx=partner(me, j))
            )

    def send_far(p):
        for j in ORDER:
            stage[p, LINKS + j, :, :WIDE] = ay[p][0, far_block[j]]
            stage[p, LINKS + j, :, WIDE:] = ay[p][1, far_block[j]]
            kv_copies[p].append(
                remote(
                    S_FWD + LINKS * p + j, stage.at[p, LINKS + j], phr[p].at[across],
                    ctx=partner(me, j),
                )
            )
        phr[p][across, :, :WIDE] = ay[p][0, far_block[LINKS]]
        phr[p][across, :, WIDE:] = ay[p][1, far_block[LINKS]]

    for c in kv_loads:
        c.wait()
    send_own(0)
    tail = pl.ds(BLK - PAD, PAD)
    halo_copies = []
    for n, (src, dst) in enumerate(((k_far, kpad), (v_far, vpad))):
        halo_copies += [
            remote(S_HALO + n, src.at[BLOCKS - 1, tail], dst.at[pl.ds(0, PAD)], ctx=nxt),
            remote(
                S_HALO + 2 + n, src.at[0, pl.ds(0, PAD)], dst.at[pl.ds(PAD + FRAMES, PAD)],
                ctx=prev,
            ),
        ]
    send_own(1, ORDER[:EARLY])
    w_first.wait()
    w_copies = []
    for n in range(LINKS):
        hop, other = (n + 1) // 2, (n + 1) % 2
        w_copies.append(
            remote(
                S_WG + n, w_o.at[eighth], w_o.at[eighth],
                ctx=twin if other else me, dp=(lane + hop) % N_DP,
            )
        )
    for pad, src in ((kpad, k), (vpad, v)):
        for b in range(BLOCKS):
            pad[PAD + b * BLK : PAD + (b + 1) * BLK, :] = src[b]
    for dst, src in ((pk, phk), (pv, phv)):
        ph_tmp[...] = jnp.zeros_like(ph_tmp)
        ph_tmp[2 * PHC : 2 * PHC + PH, :] = src[...]
        dst[...] = ph_tmp[pl.ds(pl.multiple_of(me * PHC, PHC), PH_ROWS), :]
    dpad[...] = jnp.zeros_like(dpad)
    dph[...] = jnp.zeros_like(dph)
    run[NONE] = jnp.zeros((BLK, 2 * WIDE), F32)
    for c in loads:
        c.wait()

    def each_block(body):
        def step(i, _):
            body(pl.ds(pl.multiple_of(i * BLK, BLK), BLK))
            return 0

        lax.fori_loop(0, BLOCKS, step, 0)

    def own_part(rows):
        part[rows, :] = dot(cot_v[rows, :], w_m[...], NT)

    each_block(own_part)
    for c in ay_copies[0]:
        c.wait()
    ay_copies.append(across_copies(1))
    send_far(0)
    send_own(1, ORDER[EARLY:])
    for c in w_copies:
        c.wait()

    def other_part(rows):
        p_out[rows, :] = dot(cot_v[rows, :], w_o[...], NT).astype(BF16)

    each_block(other_part)
    p_copy = remote(S_P, p_out, p_in, head=1 - head)
    for c in ay_copies[1]:
        c.wait()
    send_far(1)
    p_copy.wait()

    def whole_grad(rows):
        grad[rows, :] = (part[rows, :] + p_in[rows, :].astype(F32)).astype(BF16)

    each_block(whole_grad)
    for c in halo_copies:
        c.wait()

    rate = DH ** (-0.5)
    sources = [tbl[e % SLOTS, me * BLOCKS + e // SLOTS] // BLOCKS for e in range(NONE)]

    def attend(p):
        lanes = slice(p * WIDE, (p + 1) * WIDE)
        klanes = slice(p * 2 * WIDE, p * 2 * WIDE + WIDE)
        vlanes = slice(p * 2 * WIDE + WIDE, (p + 1) * 2 * WIDE)

        def block(i, _):
            rows = pl.ds(pl.multiple_of(i * BLK, BLK), BLK)
            wide = pl.ds(pl.multiple_of(i * BLK, BLK), 2 * BLK)
            row = lax.broadcasted_iota(jnp.int32, (2 * BLK, BLK), 0)
            col = lax.broadcasted_iota(jnp.int32, (2 * BLK, BLK), 1)
            pos = first + i * BLK - PAD + row
            seen = (jnp.abs(col - row + PAD) <= HALF_BAND) & (pos >= 0) & (pos < SEQ)
            bias = jnp.where(seen, 0.0, MASKED).astype(F32)
            band_bias[...] = jnp.concatenate([bias, bias], axis=1)
            phone = me * PHC - 2 * PHC + lax.broadcasted_iota(jnp.int32, (PH_ROWS, BLK), 0)
            near_by = jnp.abs(phone - align[0:1, rows]) <= PH_HALF
            near_by = near_by & (phone >= 0) & (phone < PH)
            bias = jnp.where(near_by, 0.0, MASKED).astype(F32)
            ph_bias[...] = jnp.concatenate([bias, bias], axis=1)
            n_used = count[0, i]
            named = [tbl[n, me * BLOCKS + i] // BLOCKS for n in range(SLOTS)]
            slot_bias = [jnp.where(n < n_used, 0.0, MASKED).astype(F32) for n in range(SLOTS)]
            qbd = two_heads(q_v[rows, lanes])
            g2 = grad[rows, lanes]
            gbd = two_heads(g2)

            def keys(c, side):
                own_pad, ph_win = ((kpad, pk), (vpad, pv))[side]
                where = slice(side * WIDE, (side + 1) * WIDE)
                if c == 0:
                    return own_pad[wide, lanes]
                if c == 3:
                    return ph_win[:, lanes]
                return jnp.concatenate(
                    [phr[p][named[2 * c - 2], :, where], phr[p][named[2 * c - 1], :, where]], axis=0
                )

            sizes = (2 * BLK, 2 * BLK, 2 * BLK, PH_ROWS)
            start = (0, 2 * BLK, 4 * BLK, 6 * BLK)
            top = jnp.full((1, 2 * BLK), -3e38, F32)
            for c in range(4):
                s = dot(keys(c, 0), qbd, NT) * (rate * LOG2E)
                if c == 0:
                    s = s + band_bias[...]
                elif c == 3:
                    s = s + ph_bias[...]
                else:
                    s = jnp.concatenate(
                        [s[:BLK] + slot_bias[2 * c - 2], s[BLK:] + slot_bias[2 * c - 1]], axis=0
                    )
                s_buf[start[c] : start[c] + sizes[c], :] = s
                top = jnp.maximum(top, jnp.max(s, axis=0, keepdims=True))
            total = jnp.zeros((1, 2 * BLK), F32)
            for c in range(4):
                at = slice(start[c], start[c] + sizes[c])
                e = jnp.exp2(s_buf[at, :] - top)
                s_buf[at, :] = e
                total = total + jnp.sum(e, axis=0, keepdims=True)
            inverse = 1.0 / total
            mixed = jnp.zeros((2 * BLK, WIDE), F32)
            for c in range(4):
                at = slice(start[c], start[c] + sizes[c])
                prob = s_buf[at, :] * inverse
                s_buf[at, :] = prob
                half = prob.astype(BF16)
                p_buf[at, :] = half
                mixed = mixed + dot(half, keys(c, 1), TN)
            a2 = jnp.concatenate([mixed[:BLK, :DH], mixed[BLK:, DH:]], axis=1).astype(BF16)
            att[rows, lanes] = a2
            product = g2.astype(F32) * a2.astype(F32)
            delta = jnp.concatenate(
                [
                    jnp.sum(product[:, :DH].T, axis=0, keepdims=True),
                    jnp.sum(product[:, DH:].T, axis=0, keepdims=True),
                ],
                axis=1,
            )
            dq2 = jnp.zeros((2 * BLK, WIDE), F32)
            for c in range(4):
                at = slice(start[c], start[c] + sizes[c])
                d_weight = dot(keys(c, 1), gbd, NT)
                ds = (s_buf[at, :] * (d_weight - delta) * rate).astype(BF16)
                dq2 = dq2 + dot(ds, keys(c, 0), TN)
                dk2 = dot(ds, qbd, NN)
                dv2 = dot(p_buf[at, :], gbd, NN)
                if c == 0:
                    dpad[wide, klanes] += dk2
                    dpad[wide, vlanes] += dv2
                elif c == 3:
                    dph[:, klanes] += dk2
                    dph[:, vlanes] += dv2
                else:
                    for n in range(2):
                        slot = 2 * c - 2 + n
                        here = i * SLOTS + slot
                        before = NONE
                        for e in range(NONE):
                            same = (sources[e] == named[slot]) & (here > e)
                            before = jnp.where(same, e, before)
                        half_rows = slice(n * BLK, (n + 1) * BLK)
                        run[here, :, :WIDE] = dk2[half_rows] + run[before, :, :WIDE]
                        run[here, :, WIDE:] = dv2[half_rows] + run[before, :, WIDE:]
            dq[rows, lanes] = jnp.concatenate([dq2[:BLK, :DH], dq2[BLK:, DH:]], axis=1).astype(BF16)
            return 0

        lax.fori_loop(0, BLOCKS, block, 0)

    def grads_of(owner):
        last = NONE
        for e in range(NONE):
            last = jnp.where(sources[e] == owner, e, last)
        return run[last].astype(BF16)

    to_relay, straight, att_copies = [{}, {}], [{}, {}], []

    def collect(p):
        for j in ORDER:
            to = partner(me, j)
            g[p, j] = grads_of(flip_y(to))
            to_relay[p][j] = remote(
                S_R + LINKS * p + j, g.at[p, j], relayed.at[p, j], ctx=to
            )
        lanes = pl.ds(p * WIDE, WIDE)
        att_copies.append(
            remote(S_ATT + p, att.at[:, lanes], att_o.at[:, lanes], head=1 - head)
        )
        relayed[p, LINKS] = grads_of(across)
        for j in ORDER:
            g[p, LINKS + j] = grads_of(partner(me, j))

    def send_straight(p):
        for j in ORDER:
            straight[p][j] = remote(
                S_D + LINKS * p + j, g.at[p, LINKS + j], direct.at[p, j], ctx=partner(me, j)
            )

    for c in kv_copies[0]:
        c.wait()
    attend(0)
    collect(0)
    for c in kv_copies[1]:
        c.wait()
    attend(1)
    collect(1)
    send_straight(0)
    rims[0] = dpad[:PAD, :].astype(BF16)
    rims[1] = dpad[PAD + FRAMES :, :].astype(BF16)
    rim_copies = [
        remote(S_RIM, rims.at[0], rims_in.at[0], ctx=prev),
        remote(S_RIM + 1, rims.at[1], rims_in.at[1], ctx=nxt),
    ]
    ph_copies = []
    for n, (chunk, by) in enumerate(((0, -2), (1, -1), (3, 1), (4, 2))):
        ph_out[n] = dph[chunk * PHC : (chunk + 1) * PHC, :].astype(BF16)
        ph_copies.append(remote(S_PHC + n, ph_out.at[n], ph_in.at[n], ctx=(me + N_CTX + by) % N_CTX))

    def slabs(features, side):
        def step(n, _):
            cols = pl.ds(pl.multiple_of(n * BLK, BLK), BLK)
            piece = dot(cot_v[:, cols], features[...], TN).astype(BF16)
            at = side * (OCT // 2) + n // 2
            for d in range(N_DP):
                dwx[n % 2, d, at] = piece[d * SLAB : (d + 1) * SLAB]
            return 0

        lax.fori_loop(0, OCT, step, 0)

    weights_far, weights_own = [], []
    for u in [sender(me, j) for j in range(LINKS)] + [me]:
        for owner, weights in ((across, weights_far), (me, weights_own)):
            block, found = named_block(tbl, u, owner)
            weights.append(
                [jnp.where((block == b) & (found == 1), 1.0, 0.0).astype(F32) for b in range(BLOCKS)]
            )
    relay_copies = [[], []]

    def relay(p):
        for j in ORDER:
            to_relay[p][j].wait()
        for b in range(BLOCKS):

            def add(i, _, b=b):
                rows = pl.ds(pl.multiple_of(i * STEP, STEP), STEP)
                t = relayed[p, 0, rows, :].astype(F32) * weights_far[0][b]
                for n in range(1, LINKS + 1):
                    t = t + relayed[p, n, rows, :].astype(F32) * weights_far[n][b]
                rsum[p, b, rows, :] = t.astype(BF16)
                return 0

            lax.fori_loop(0, BLK // STEP, add, 0)
            relay_copies[p].append(
                remote(S_Y + BLOCKS * p + b, rsum.at[p, b], summed.at[p, b], ctx=across)
            )

    slabs(att, head)
    relay(0)
    for c in att_copies:
        c.wait()
    slabs(att_o, 1 - head)
    dw_core = remote(S_DWC, dwx.at[1 - parity], dwc, ctx=twin)

    for c in ph_copies:
        c.wait()
    total = dph[2 * PHC : 3 * PHC, :]
    for n, by in ((0, 2), (1, 1), (2, -1), (3, -2)):
        origin = me + by
        there = (origin >= 0) & (origin < N_CTX)
        total = total + jnp.where(there, ph_in[n].astype(F32), 0.0)
    ph_mine[...] = total.astype(BF16)
    ph_all[parity, me // 2] = ph_mine[...]
    ph_bcast = [
        remote(S_PHB + s - 1, ph_mine, ph_all.at[parity, me // 2], ctx=(me + 2 * s) % N_CTX)
        for s in range(1, OCT)
    ]
    dw_core.wait()

    def over_core(i, _):
        for d in range(N_DP):
            dws[d, i] = (dwx[parity, d, i].astype(F32) + dwc[d, i].astype(F32)).astype(BF16)
        return 0

    lax.fori_loop(0, OCT, over_core, 0)
    dw_x = [
        remote(S_DWX + s - 1, dws.at[(lane + s) % N_DP], dwr.at[s - 1], dp=(lane + s) % N_DP)
        for s in range(1, N_DP)
    ]
    relay(1)
    send_straight(1)

    def project(rows):
        t = dot(att[rows, :], w_m[...], NN) + dot(att_o[rows, :], w_o[...], NN)
        layer[rows, :] = t.astype(BF16)

    each_block(project)
    for c in ph_bcast:
        c.wait()
    ph_core = remote(S_PHX, ph_all.at[parity], ph_all.at[parity], ctx=twin)
    for c in dw_x:
        c.wait()

    def over_dp(i, _):
        t = dws[lane, i].astype(F32)
        for s in range(N_DP - 1):
            t = t + dwr[s, i].astype(F32)
        dwm[i] = t.astype(BF16)
        return 0

    lax.fori_loop(0, OCT, over_dp, 0)
    dw_t = []
    for s in range(1, OCT):
        to = (me + 2 * s) % N_CTX
        dw_t.append(remote(S_DWT + s - 1, dwm.at[to // 2], dwl.at[s - 1], ctx=to))

    def finish(p):
        for j in ORDER:
            straight[p][j].wait()
        lanes = slice(p * WIDE, (p + 1) * WIDE)
        both = slice(p * 2 * WIDE, (p + 1) * 2 * WIDE)
        for b in range(BLOCKS):
            relay_copies[p][b].wait()

            def add(i, _, b=b):
                rows = pl.ds(pl.multiple_of(i * STEP, STEP), STEP)
                here = pl.ds(pl.multiple_of(b * BLK + i * STEP, STEP), STEP)
                there = pl.ds(pl.multiple_of(PAD + b * BLK + i * STEP, STEP), STEP)
                t = dpad[there, both] + summed[p, b, rows, :].astype(F32)
                for n in range(LINKS):
                    t = t + direct[p, n, rows, :].astype(F32) * weights_own[n][b]
                dk[here, lanes] = t[:, :WIDE].astype(BF16)
                dv[here, lanes] = t[:, WIDE:].astype(BF16)
                return 0

            lax.fori_loop(0, BLK // STEP, add, 0)

    for c in rim_copies:
        c.wait()
    low, high = slice(PAD, 2 * PAD), slice(FRAMES, FRAMES + PAD)
    dpad[high, :] += jnp.where(me < N_CTX - 1, rims_in[0].astype(F32), 0.0)
    dpad[low, :] += jnp.where(me > 0, rims_in[1].astype(F32), 0.0)
    finish(0)
    for c in dw_t:
        c.wait()
    t = dwm[me // 2].astype(F32)
    for s in range(OCT - 1):
        t = t + dwl[s].astype(F32)
    dwe[...] = t * (1.0 / math.sqrt(N_DP * SEQ))
    dw_last = remote(S_DWL, dwe, dwf, ctx=(me + OCT) % N_CTX, head=1 - head)
    ph_core.wait()
    for i in range(N_CTX):
        at = slice(i * PHC, (i + 1) * PHC)
        for p in range(PAIRS):
            lanes = slice(p * WIDE, (p + 1) * WIDE)
            here = p * 2 * WIDE
            dphk[at, lanes] = ph_all[i % 2, i // 2, :, here : here + WIDE]
            dphv[at, lanes] = ph_all[i % 2, i // 2, :, here + WIDE : here + 2 * WIDE]
    dw_last.wait()
    dw[...] = jnp.where(me // OCT == head, dwe[...], dwf[...])
    finish(1)


def layer_call(tbl, count, align, k, v, q, cot, w, phk, phv):
    scratch = (
        ((BLOCKS, BLK, FEAT), BF16),
        ((BLOCKS, BLK, FEAT), BF16),
        ((PAIRS, 2 * LINKS, BLK, 2 * WIDE), BF16),
        ((2, BLOCKS, BLK, WIDE), BF16),
        ((2, BLOCKS, BLK, WIDE), BF16),
        ((N_CTX, BLK, 2 * WIDE), BF16),
        ((N_CTX, BLK, 2 * WIDE), BF16),
        ((FRAMES, HALF), BF16),
        ((FEAT, HALF), BF16),
        ((FEAT, HALF), BF16),
        ((FRAMES, FEAT), F32),
        ((FRAMES, FEAT), BF16),
        ((FRAMES, FEAT), BF16),
        ((FRAMES, FEAT), BF16),
        ((FRAMES, FEAT), BF16),
        ((FRAMES + 2 * PAD, FEAT), BF16),
        ((FRAMES + 2 * PAD, FEAT), BF16),
        ((PH_ROWS, FEAT), BF16),
        ((PH_ROWS, FEAT), BF16),
        ((PH + 2 * PHC + PH_ROWS, FEAT), BF16),
        ((FRAMES + 2 * PAD, 2 * FEAT), F32),
        ((PH_ROWS, 2 * FEAT), F32),
        ((NONE + 1, BLK, 2 * WIDE), F32),
        ((PAIRS, 2 * LINKS, BLK, 2 * WIDE), BF16),
        ((KEYS, 2 * BLK), F32),
        ((KEYS, 2 * BLK), BF16),
        ((2 * BLK, 2 * BLK), F32),
        ((PH_ROWS, 2 * BLK), F32),
        ((PAIRS, LINKS + 1, BLK, 2 * WIDE), BF16),
        ((PAIRS, LINKS, BLK, 2 * WIDE), BF16),
        ((PAIRS, BLOCKS, BLK, 2 * WIDE), BF16),
        ((PAIRS, BLOCKS, BLK, 2 * WIDE), BF16),
        ((2, PAD, 2 * FEAT), BF16),
        ((2, PAD, 2 * FEAT), BF16),
        ((4, PHC, 2 * FEAT), BF16),
        ((4, PHC, 2 * FEAT), BF16),
        ((PHC, 2 * FEAT), BF16),
        ((2, OCT, PHC, 2 * FEAT), BF16),
        ((FRAMES, FEAT), BF16),
        ((FRAMES, FEAT), BF16),
        ((2, N_DP, OCT, SLAB, FEAT), BF16),
        ((N_DP, OCT, SLAB, FEAT), BF16),
        ((N_DP, OCT, SLAB, FEAT), BF16),
        ((N_DP - 1, OCT, SLAB, FEAT), BF16),
        ((OCT, SLAB, FEAT), BF16),
        ((OCT - 1, SLAB, FEAT), BF16),
        ((SLAB, FEAT), F32),
        ((SLAB, FEAT), F32),
    )
    return pl.pallas_call(
        layer_kernel,
        out_shape=(
            jax.ShapeDtypeStruct((FRAMES, HALF), BF16),
            jax.ShapeDtypeStruct((FRAMES, FEAT), BF16),
            jax.ShapeDtypeStruct((FRAMES, FEAT), BF16),
            jax.ShapeDtypeStruct((FRAMES, FEAT), BF16),
            jax.ShapeDtypeStruct((PH, FEAT), BF16),
            jax.ShapeDtypeStruct((PH, FEAT), BF16),
            jax.ShapeDtypeStruct((SLAB, FEAT), F32),
        ),
        in_specs=[SMEM, SMEM, VMEM, ANY, ANY, ANY, ANY, ANY, VMEM, VMEM],
        out_specs=(VMEM,) * 7,
        scratch_shapes=[pltpu.VMEM(shape, kind) for shape, kind in scratch]
        + [
            pltpu.SemaphoreType.DMA((S_ALL,)),
            pltpu.SemaphoreType.DMA((S_ALL,)),
            pltpu.SemaphoreType.DMA((5,)),
        ],
        compiler_params=pltpu.CompilerParams(
            collective_id=0, has_side_effects=True, vmem_limit_bytes=BIG
        ),
        name="layer",
    )(
        tbl, count, align, k.reshape(BLOCKS, BLK, FEAT), v.reshape(BLOCKS, BLK, FEAT),
        q, cot, w, phk, phv,
    )


def hand_on_kernel(*refs):
    n = len(refs) // 2
    for i in range(n):
        refs[n + i][...] = refs[i][...]


def hand_on(*arrays):
    parts = 4
    specs = [pl.BlockSpec((a.shape[0] // parts, a.shape[1]), lambda i: (i, 0)) for a in arrays]
    return pl.pallas_call(
        hand_on_kernel,
        out_shape=tuple(jax.ShapeDtypeStruct(a.shape, a.dtype) for a in arrays),
        grid=(parts,),
        in_specs=specs,
        out_specs=tuple(specs),
        name="hand_on",
    )(*arrays)


def local(q, k, v, cot, w, phk, phv, tbl, count, align):
    q, k, v, cot, phk, phv, tbl = q[0], k[0], v[0], cot[0], phk[0], phv[0], tbl[0].T
    layer, dq, dk, dv, dphk, dphv, dw = layer_call(
        tbl, count, align, k, v, q, cot, w, phk, phv
    )
    layer, dq, dk, dv, dphk, dphv, dw = hand_on(layer, dq, dk, dv, dphk, dphv, dw)
    return (layer[None], dq[None], dk[None], dv[None], dphk[None], dphv[None], dw.T)


def solution(mesh):
    placed = (
        P("dp", "ctx", "head"),
        P("dp", "ctx", "head"),
        P("dp", "ctx", "head"),
        P("dp", "ctx", "head"),
        P("head", None),
        P("dp", None, "head"),
        P("dp", None, "head"),
        P("dp", None, None),
        P("dp", "ctx"),
        P("dp", "ctx"),
    )
    return jax.shard_map(
        local,
        mesh=mesh,
        in_specs=placed,
        out_specs=(
            P("dp", "ctx", "head"),
            P("dp", "ctx", "head"),
            P("dp", "ctx", "head"),
            P("dp", "ctx", "head"),
            P("dp", None, "head"),
            P("dp", None, "head"),
            P("head", ("ctx", "dp")),
        ),
        check_vma=False,
    )
```

```python
import functools
import math

import jax
import jax.numpy as jnp
from jax import lax
from jax.experimental import pallas as pl
from jax.experimental.pallas import tpu as pltpu
from jax.sharding import PartitionSpec as P

MESH = pl.DeviceIdType.MESH
ANY = pl.BlockSpec(memory_space=pl.ANY)
VMEM = pl.BlockSpec(memory_space=pltpu.VMEM)
SMEM = pl.BlockSpec(memory_space=pltpu.SMEM)
BF16 = jnp.bfloat16
F32 = jnp.float32

DH = 128
BLK = 128
HALF_BAND = 64
SLOTS = 4
PH_HALF = 16
PH = 256
N_CTX = 16
N_DP = 4
FRAMES = 512
BLOCKS = 4
FEAT = 512
MODEL = 2048
HALF = 1024
SEQ = FRAMES * N_CTX
PHC = 16
MASKED = -1e30
LOG2E = 1.4426950408889634
LINKS = 7
BIG = 60 * 1024 * 1024

NT = (((1,), (1,)), ((), ()))
NN = (((1,), (0,)), ((), ()))
TN = (((0,), (0,)), ((), ()))


def dot(a, b, dims):
    return lax.dot_general(a, b, dims, preferred_element_type=F32)


def flip_core(c):
    return c + 1 - 2 * (c % 2)


def flip_y(c):
    return c + 2 - 4 * ((c // 2) % 2)


def partner(me, j):
    if j == 0:
        return flip_core(me)
    hop, other = 1 + (j - 1) // 2, (j - 1) % 2
    low = me % 4
    low = flip_core(low) if other else low
    return ((me // 4 + hop) % 4) * 4 + low


def sender(me, j):
    if j == 0:
        return flip_core(me)
    hop, other = 1 + (j - 1) // 2, (j - 1) % 2
    low = me % 4
    low = flip_core(low) if other else low
    return ((me // 4 + 4 - hop) % 4) * 4 + low


ORDER = (3, 4, 1, 2, 5, 6, 0)


def named_block(tbl, user, owner):
    block, found = 0, 0
    for e in range(BLOCKS * SLOTS):
        entry = tbl[e % SLOTS, user * BLOCKS + e // SLOTS]
        hit = entry // BLOCKS == owner
        block = jnp.where(hit, entry % BLOCKS, block)
        found = jnp.where(hit, 1, found)
    return block, found


PAIRS = 2
WIDE = 2 * DH
PH_ROWS = 128
PAD = HALF_BAND
NONE = BLOCKS * SLOTS
SLAB = 32
OCT = N_CTX // 2
W_PART = FEAT // (2 * N_DP)
STEP = 16
EARLY = 3
KEYS = 6 * BLK + PH_ROWS

S_W, S_WG, S_AY, S_P, S_HALO, S_OWN, S_FWD = 0, 1, 8, 12, 13, 17, 31
S_R, S_D, S_Y, S_ATT, S_RIM, S_PHC, S_PHB, S_PHX = 45, 59, 73, 81, 83, 85, 89, 96
S_DWC, S_DWX, S_DWT, S_DWL, S_P1, S_ALL = 97, 98, 101, 108, 109, 110


def two_heads(x):
    zero = jnp.zeros((BLK, DH), x.dtype)
    top = jnp.concatenate([x[:, :DH], zero], axis=1)
    low = jnp.concatenate([zero, x[:, DH:]], axis=1)
    return jnp.concatenate([top, low], axis=0)


def layer_kernel(
    tbl, count, align, k_far, v_far, q, cot, w, phk, phv,
    layer_hbm, dq_hbm, dk_hbm, dv_hbm, dphk_hbm, dphv_hbm, dw_hbm,
    layer, dq, dk, dv, dphk, dphv, dw, k, v, stage, ay0, ay1, phr0, phr1, cot_v, w_m, w_o, part, p_out, p_in, grad, q_v, kpad, vpad, pk, pv, ph_tmp,
    dpad, dph, run, g, s_buf, p_buf, band_bias, ph_bias, relayed, direct, rsum, summed,
    rims, rims_in, ph_out, ph_in, ph_mine, ph_all, att, att_o,
    dwx, dwc, dws, dwr, dwm, dwl, dwe, dwf, send, recv, near,
):
    ay, phr = (ay0, ay1), (phr0, phr1)
    me, head, lane = lax.axis_index("ctx"), lax.axis_index("head"), lax.axis_index("dp")
    across, twin = flip_y(me), flip_core(me)
    prev, nxt = (me + N_CTX - 1) % N_CTX, (me + 1) % N_CTX
    parity = me % 2
    first = me * FRAMES
    mine = pl.ds(pl.multiple_of(head * HALF, HALF), HALF)
    theirs = pl.ds(pl.multiple_of((1 - head) * HALF, HALF), HALF)
    loads = [
        pltpu.make_async_copy(cot, cot_v, near.at[0]),
        pltpu.make_async_copy(w.at[:, mine], w_m, near.at[1]),
        pltpu.make_async_copy(q, q_v, near.at[2]),
    ]
    kv_loads = [
        pltpu.make_async_copy(k_far, k, near.at[3]),
        pltpu.make_async_copy(v_far, v, near.at[4]),
    ]
    for c in kv_loads + loads:
        c.start()

    results = []

    def deliver(src, dst):
        c = pltpu.make_async_copy(src, dst, near.at[5 + len(results)])
        c.start()
        results.append(c)

    def remote(i, src, dst, **to):
        c = pltpu.make_async_remote_copy(
            src, dst, send.at[i], recv.at[i], device_id=to, device_id_type=MESH
        )
        c.start()
        return c

    mesh_peers = [{"ctx": (me + s) % N_CTX} for s in range(1, N_CTX)]
    mesh_peers += [{"dp": (lane + s) % N_DP} for s in range(1, N_DP)]
    mesh_peers += [{"head": 1 - head}, {"ctx": (me + OCT) % N_CTX, "head": 1 - head}]
    barrier = pltpu.get_barrier_semaphore()
    for device in mesh_peers:
        pl.semaphore_signal(barrier, inc=1, device_id=device, device_id_type=MESH)
    own_block = {j: named_block(tbl, partner(me, j), me)[0] for j in ORDER}
    far_block = {j: named_block(tbl, partner(me, j), across)[0] for j in ORDER}
    far_block[LINKS] = named_block(tbl, me, across)[0]
    pl.semaphore_wait(barrier, len(mesh_peers))

    def eighth(of):
        return w_o.at[pl.ds(pl.multiple_of((of * 2 + parity) * W_PART, W_PART), W_PART)]

    w_rows = pl.ds(pl.multiple_of((lane * 2 + parity) * W_PART, W_PART), W_PART)
    w_first = remote(S_W, w.at[w_rows, theirs], eighth(lane), head=1 - head)

    def across_copy(p, n):
        lanes = pl.ds(p * WIDE, WIDE)
        src = (k_far, v_far)[n]
        return remote(S_AY + 2 * p + n, src.at[:, :, lanes], ay[p].at[n], ctx=across)

    ay_copies = [[across_copy(0, 0)], []]
    kv_copies = [[], []]

    def send_own(p, these=ORDER):
        for j in these:
            lanes = slice(p * WIDE, (p + 1) * WIDE)
            stage[p, j, :, :WIDE] = k[own_block[j], :, lanes]
            stage[p, j, :, WIDE:] = v[own_block[j], :, lanes]
            kv_copies[p].append(
                remote(S_OWN + LINKS * p + j, stage.at[p, j], phr[p].at[me], ctx=partner(me, j))
            )

    def send_far(p):
        for j in ORDER:
            stage[p, LINKS + j, :, :WIDE] = ay[p][0, far_block[j]]
            stage[p, LINKS + j, :, WIDE:] = ay[p][1, far_block[j]]
            kv_copies[p].append(
                remote(
                    S_FWD + LINKS * p + j, stage.at[p, LINKS + j], phr[p].at[across],
                    ctx=partner(me, j),
                )
            )
        phr[p][across, :, :WIDE] = ay[p][0, far_block[LINKS]]
        phr[p][across, :, WIDE:] = ay[p][1, far_block[LINKS]]

    for c in kv_loads:
        c.wait()
    send_own(0)
    w_first.wait()
    w_x = [remote(S_WG + s - 1, eighth(lane), eighth(lane), dp=(lane + s) % N_DP) for s in range(1, N_DP)]
    w_core = [remote(S_WG + N_DP - 1, eighth(lane), eighth(lane), ctx=twin)]
    ay_copies[0].append(across_copy(0, 1))
    tail = pl.ds(BLK - PAD, PAD)
    halo_copies = []
    for n, (src, dst) in enumerate(((k_far, kpad), (v_far, vpad))):
        halo_copies += [
            remote(S_HALO + n, src.at[BLOCKS - 1, tail], dst.at[pl.ds(0, PAD)], ctx=nxt),
            remote(
                S_HALO + 2 + n, src.at[0, pl.ds(0, PAD)], dst.at[pl.ds(PAD + FRAMES, PAD)],
                ctx=prev,
            ),
        ]
    send_own(1, ORDER[:EARLY])
    for pad, src in ((kpad, k), (vpad, v)):
        for b in range(BLOCKS):
            pad[PAD + b * BLK : PAD + (b + 1) * BLK, :] = src[b]
    for dst, src in ((pk, phk), (pv, phv)):
        ph_tmp[...] = jnp.zeros_like(ph_tmp)
        ph_tmp[2 * PHC : 2 * PHC + PH, :] = src[...]
        dst[...] = ph_tmp[pl.ds(pl.multiple_of(me * PHC, PHC), PH_ROWS), :]
    dpad[...] = jnp.zeros_like(dpad)
    dph[...] = jnp.zeros_like(dph)
    run[NONE] = jnp.zeros((BLK, 2 * WIDE), F32)
    for c in loads:
        c.wait()

    def each_block(body):
        def step(i, _):
            body(pl.ds(pl.multiple_of(i * BLK, BLK), BLK))
            return 0

        lax.fori_loop(0, BLOCKS, step, 0)

    def own_part(rows):
        part[rows, :] = dot(cot_v[rows, :], w_m[...], NT)

    each_block(own_part)
    for n in range(1, N_DP):
        w_x[n - 1].wait()
        came = eighth((lane + N_DP - n) % N_DP)
        w_core.append(remote(S_WG + N_DP - 1 + n, came, came, ctx=twin))
    for c in ay_copies[0]:
        c.wait()
    ay_copies[1] = [across_copy(1, 0), across_copy(1, 1)]
    send_far(0)
    for c in w_core:
        c.wait()

    def other_part(p):
        lanes = slice(p * WIDE, (p + 1) * WIDE)

        def step(rows):
            p_out[rows, lanes] = dot(cot_v[rows, :], w_o[lanes, :], NT).astype(BF16)

        each_block(step)

    def send_part(p):
        lanes = pl.ds(p * WIDE, WIDE)
        return remote((S_P, S_P1)[p], p_out.at[:, lanes], p_in.at[:, lanes], head=1 - head)

    other_part(0)
    p_copies = [send_part(0)]
    send_own(1, ORDER[EARLY:])
    other_part(1)
    for c in ay_copies[1]:
        c.wait()
    send_far(1)
    p_copies.append(send_part(1))

    def whole_grad(p):
        lanes = slice(p * WIDE, (p + 1) * WIDE)
        p_copies[p].wait()

        def step(rows):
            grad[rows, lanes] = (part[rows, lanes] + p_in[rows, lanes].astype(F32)).astype(BF16)

        each_block(step)

    whole_grad(0)
    for c in halo_copies:
        c.wait()

    rate = DH ** (-0.5)
    sources = [tbl[e % SLOTS, me * BLOCKS + e // SLOTS] // BLOCKS for e in range(NONE)]

    def attend(p):
        lanes = slice(p * WIDE, (p + 1) * WIDE)
        klanes = slice(p * 2 * WIDE, p * 2 * WIDE + WIDE)
        vlanes = slice(p * 2 * WIDE + WIDE, (p + 1) * 2 * WIDE)

        def block(i, _):
            rows = pl.ds(pl.multiple_of(i * BLK, BLK), BLK)
            wide = pl.ds(pl.multiple_of(i * BLK, BLK), 2 * BLK)
            row = lax.broadcasted_iota(jnp.int32, (2 * BLK, BLK), 0)
            col = lax.broadcasted_iota(jnp.int32, (2 * BLK, BLK), 1)
            pos = first + i * BLK - PAD + row
            seen = (jnp.abs(col - row + PAD) <= HALF_BAND) & (pos >= 0) & (pos < SEQ)
            bias = jnp.where(seen, 0.0, MASKED).astype(F32)
            band_bias[...] = jnp.concatenate([bias, bias], axis=1)
            phone = me * PHC - 2 * PHC + lax.broadcasted_iota(jnp.int32, (PH_ROWS, BLK), 0)
            near_by = jnp.abs(phone - align[0:1, rows]) <= PH_HALF
            near_by = near_by & (phone >= 0) & (phone < PH)
            bias = jnp.where(near_by, 0.0, MASKED).astype(F32)
            ph_bias[...] = jnp.concatenate([bias, bias], axis=1)
            n_used = count[0, i]
            named = [tbl[n, me * BLOCKS + i] // BLOCKS for n in range(SLOTS)]
            slot_bias = [jnp.where(n < n_used, 0.0, MASKED).astype(F32) for n in range(SLOTS)]
            qbd = two_heads(q_v[rows, lanes])
            g2 = grad[rows, lanes]
            gbd = two_heads(g2)

            def keys(c, side):
                own_pad, ph_win = ((kpad, pk), (vpad, pv))[side]
                where = slice(side * WIDE, (side + 1) * WIDE)
                if c == 0:
                    return own_pad[wide, lanes]
                if c == 3:
                    return ph_win[:, lanes]
                return jnp.concatenate(
                    [phr[p][named[2 * c - 2], :, where], phr[p][named[2 * c - 1], :, where]], axis=0
                )

            sizes = (2 * BLK, 2 * BLK, 2 * BLK, PH_ROWS)
            start = (0, 2 * BLK, 4 * BLK, 6 * BLK)
            top = jnp.full((1, 2 * BLK), -3e38, F32)
            for c in range(4):
                s = dot(keys(c, 0), qbd, NT) * (rate * LOG2E)
                if c == 0:
                    s = s + band_bias[...]
                elif c == 3:
                    s = s + ph_bias[...]
                else:
                    s = jnp.concatenate(
                        [s[:BLK] + slot_bias[2 * c - 2], s[BLK:] + slot_bias[2 * c - 1]], axis=0
                    )
                s_buf[start[c] : start[c] + sizes[c], :] = s
                top = jnp.maximum(top, jnp.max(s, axis=0, keepdims=True))
            total = jnp.zeros((1, 2 * BLK), F32)
            for c in range(4):
                at = slice(start[c], start[c] + sizes[c])
                e = jnp.exp2(s_buf[at, :] - top)
                s_buf[at, :] = e
                total = total + jnp.sum(e, axis=0, keepdims=True)
            inverse = 1.0 / total
            mixed = jnp.zeros((2 * BLK, WIDE), F32)
            for c in range(4):
                at = slice(start[c], start[c] + sizes[c])
                prob = s_buf[at, :] * inverse
                s_buf[at, :] = prob
                half = prob.astype(BF16)
                p_buf[at, :] = half
                mixed = mixed + dot(half, keys(c, 1), TN)
            a2 = jnp.concatenate([mixed[:BLK, :DH], mixed[BLK:, DH:]], axis=1).astype(BF16)
            att[rows, lanes] = a2
            product = g2.astype(F32) * a2.astype(F32)
            delta = jnp.concatenate(
                [
                    jnp.sum(product[:, :DH].T, axis=0, keepdims=True),
                    jnp.sum(product[:, DH:].T, axis=0, keepdims=True),
                ],
                axis=1,
            )
            dq2 = jnp.zeros((2 * BLK, WIDE), F32)
            for c in range(4):
                at = slice(start[c], start[c] + sizes[c])
                d_weight = dot(keys(c, 1), gbd, NT)
                ds = (s_buf[at, :] * (d_weight - delta) * rate).astype(BF16)
                dq2 = dq2 + dot(ds, keys(c, 0), TN)
                dk2 = dot(ds, qbd, NN)
                dv2 = dot(p_buf[at, :], gbd, NN)
                if c == 0:
                    dpad[wide, klanes] += dk2
                    dpad[wide, vlanes] += dv2
                elif c == 3:
                    dph[:, klanes] += dk2
                    dph[:, vlanes] += dv2
                else:
                    for n in range(2):
                        slot = 2 * c - 2 + n
                        here = i * SLOTS + slot
                        before = NONE
                        for e in range(NONE):
                            same = (sources[e] == named[slot]) & (here > e)
                            before = jnp.where(same, e, before)
                        half_rows = slice(n * BLK, (n + 1) * BLK)
                        run[here, :, :WIDE] = dk2[half_rows] + run[before, :, :WIDE]
                        run[here, :, WIDE:] = dv2[half_rows] + run[before, :, WIDE:]
            dq[rows, lanes] = jnp.concatenate([dq2[:BLK, :DH], dq2[BLK:, DH:]], axis=1).astype(BF16)
            return 0

        lax.fori_loop(0, BLOCKS, block, 0)

    def grads_of(owner):
        last = NONE
        for e in range(NONE):
            last = jnp.where(sources[e] == owner, e, last)
        return run[last].astype(BF16)

    to_relay, straight, att_copies = [{}, {}], [{}, {}], []

    def collect(p):
        for j in ORDER:
            to = partner(me, j)
            g[p, j] = grads_of(flip_y(to))
            to_relay[p][j] = remote(
                S_R + LINKS * p + j, g.at[p, j], relayed.at[p, j], ctx=to
            )
        lanes = pl.ds(p * WIDE, WIDE)
        att_copies.append(
            remote(S_ATT + p, att.at[:, lanes], att_o.at[:, lanes], head=1 - head)
        )
        relayed[p, LINKS] = grads_of(across)
        for j in ORDER:
            g[p, LINKS + j] = grads_of(partner(me, j))

    def send_straight(p):
        for j in ORDER:
            straight[p][j] = remote(
                S_D + LINKS * p + j, g.at[p, LINKS + j], direct.at[p, j], ctx=partner(me, j)
            )

    for c in kv_copies[0]:
        c.wait()
    attend(0)
    collect(0)
    whole_grad(1)
    for c in kv_copies[1]:
        c.wait()
    send_straight(0)
    attend(1)
    collect(1)
    deliver(dq, dq_hbm)
    rims[0] = dpad[:PAD, :].astype(BF16)
    rims[1] = dpad[PAD + FRAMES :, :].astype(BF16)
    rim_copies = [
        remote(S_RIM, rims.at[0], rims_in.at[0], ctx=prev),
        remote(S_RIM + 1, rims.at[1], rims_in.at[1], ctx=nxt),
    ]
    ph_copies = []
    for n, (chunk, by) in enumerate(((0, -2), (1, -1), (3, 1), (4, 2))):
        ph_out[n] = dph[chunk * PHC : (chunk + 1) * PHC, :].astype(BF16)
        ph_copies.append(remote(S_PHC + n, ph_out.at[n], ph_in.at[n], ctx=(me + N_CTX + by) % N_CTX))

    def slabs(features, side):
        def step(n, _):
            cols = pl.ds(pl.multiple_of(n * BLK, BLK), BLK)
            piece = dot(cot_v[:, cols], features[...], TN).astype(BF16)
            at = side * (OCT // 2) + n // 2
            for d in range(N_DP):
                dwx[n % 2, d, at] = piece[d * SLAB : (d + 1) * SLAB]
            return 0

        lax.fori_loop(0, OCT, step, 0)

    weights_far, weights_own = [], []
    for u in [sender(me, j) for j in range(LINKS)] + [me]:
        for owner, weights in ((across, weights_far), (me, weights_own)):
            block, found = named_block(tbl, u, owner)
            weights.append(
                [jnp.where((block == b) & (found == 1), 1.0, 0.0).astype(F32) for b in range(BLOCKS)]
            )
    relay_copies = [[], []]

    def relay(p):
        for j in ORDER:
            to_relay[p][j].wait()
        for b in range(BLOCKS):

            def add(i, _, b=b):
                rows = pl.ds(pl.multiple_of(i * STEP, STEP), STEP)
                t = relayed[p, 0, rows, :].astype(F32) * weights_far[0][b]
                for n in range(1, LINKS + 1):
                    t = t + relayed[p, n, rows, :].astype(F32) * weights_far[n][b]
                rsum[p, b, rows, :] = t.astype(BF16)
                return 0

            lax.fori_loop(0, BLK // STEP, add, 0)
            relay_copies[p].append(
                remote(S_Y + BLOCKS * p + b, rsum.at[p, b], summed.at[p, b], ctx=across)
            )

    slabs(att, head)
    for c in att_copies:
        c.wait()
    slabs(att_o, 1 - head)
    dw_core = remote(S_DWC, dwx.at[1 - parity], dwc, ctx=twin)
    relay(0)

    for c in ph_copies:
        c.wait()
    total = dph[2 * PHC : 3 * PHC, :]
    for n, by in ((0, 2), (1, 1), (2, -1), (3, -2)):
        origin = me + by
        there = (origin >= 0) & (origin < N_CTX)
        total = total + jnp.where(there, ph_in[n].astype(F32), 0.0)
    ph_mine[...] = total.astype(BF16)
    ph_all[parity, me // 2] = ph_mine[...]
    ph_bcast = [
        remote(S_PHB + s - 1, ph_mine, ph_all.at[parity, me // 2], ctx=(me + 2 * s) % N_CTX)
        for s in range(1, OCT)
    ]
    dw_core.wait()

    def over_core(i, _):
        for d in range(N_DP):
            dws[d, i] = (dwx[parity, d, i].astype(F32) + dwc[d, i].astype(F32)).astype(BF16)
        return 0

    lax.fori_loop(0, OCT, over_core, 0)
    dw_x = [
        remote(S_DWX + s - 1, dws.at[(lane + s) % N_DP], dwr.at[s - 1], dp=(lane + s) % N_DP)
        for s in range(1, N_DP)
    ]
    relay(1)
    send_straight(1)

    def project(rows):
        t = dot(att[rows, :], w_m[...], NN) + dot(att_o[rows, :], w_o[...], NN)
        layer[rows, :] = t.astype(BF16)

    each_block(project)
    deliver(layer, layer_hbm)
    for c in ph_bcast:
        c.wait()
    ph_core = remote(S_PHX, ph_all.at[parity], ph_all.at[parity], ctx=twin)
    for c in dw_x:
        c.wait()

    def over_dp(i, _):
        t = dws[lane, i].astype(F32)
        for s in range(N_DP - 1):
            t = t + dwr[s, i].astype(F32)
        dwm[i] = t.astype(BF16)
        return 0

    lax.fori_loop(0, OCT, over_dp, 0)
    dw_t = []
    for s in range(1, OCT):
        to = (me + 2 * s) % N_CTX
        dw_t.append(remote(S_DWT + s - 1, dwm.at[to // 2], dwl.at[s - 1], ctx=to))

    def finish(p):
        for j in ORDER:
            straight[p][j].wait()
        lanes = slice(p * WIDE, (p + 1) * WIDE)
        both = slice(p * 2 * WIDE, (p + 1) * 2 * WIDE)
        for b in range(BLOCKS):
            relay_copies[p][b].wait()

            def add(i, _, b=b):
                rows = pl.ds(pl.multiple_of(i * STEP, STEP), STEP)
                here = pl.ds(pl.multiple_of(b * BLK + i * STEP, STEP), STEP)
                there = pl.ds(pl.multiple_of(PAD + b * BLK + i * STEP, STEP), STEP)
                t = dpad[there, both] + summed[p, b, rows, :].astype(F32)
                for n in range(LINKS):
                    t = t + direct[p, n, rows, :].astype(F32) * weights_own[n][b]
                dk[here, lanes] = t[:, :WIDE].astype(BF16)
                dv[here, lanes] = t[:, WIDE:].astype(BF16)
                return 0

            lax.fori_loop(0, BLK // STEP, add, 0)
        some = pl.ds(p * WIDE, WIDE)
        deliver(dk.at[:, some], dk_hbm.at[:, some])
        deliver(dv.at[:, some], dv_hbm.at[:, some])

    for c in rim_copies:
        c.wait()
    low, high = slice(PAD, 2 * PAD), slice(FRAMES, FRAMES + PAD)
    dpad[high, :] += jnp.where(me < N_CTX - 1, rims_in[0].astype(F32), 0.0)
    dpad[low, :] += jnp.where(me > 0, rims_in[1].astype(F32), 0.0)
    finish(0)
    for c in dw_t:
        c.wait()
    t = dwm[me // 2].astype(F32)
    for s in range(OCT - 1):
        t = t + dwl[s].astype(F32)
    dwe[...] = t * (1.0 / math.sqrt(N_DP * SEQ))
    dw_last = remote(S_DWL, dwe, dwf, ctx=(me + OCT) % N_CTX, head=1 - head)
    ph_core.wait()
    for i in range(N_CTX):
        at = slice(i * PHC, (i + 1) * PHC)
        for p in range(PAIRS):
            lanes = slice(p * WIDE, (p + 1) * WIDE)
            here = p * 2 * WIDE
            dphk[at, lanes] = ph_all[i % 2, i // 2, :, here : here + WIDE]
            dphv[at, lanes] = ph_all[i % 2, i // 2, :, here + WIDE : here + 2 * WIDE]
    deliver(dphk, dphk_hbm)
    deliver(dphv, dphv_hbm)
    finish(1)
    dw_last.wait()
    dw[...] = jnp.where(me // OCT == head, dwe[...], dwf[...])
    deliver(dw, dw_hbm)
    for c in results:
        c.wait()


def layer_call(tbl, count, align, k, v, q, cot, w, phk, phv):
    scratch = (
        ((FRAMES, HALF), BF16),
        ((FRAMES, FEAT), BF16),
        ((FRAMES, FEAT), BF16),
        ((FRAMES, FEAT), BF16),
        ((PH, FEAT), BF16),
        ((PH, FEAT), BF16),
        ((SLAB, FEAT), F32),
        ((BLOCKS, BLK, FEAT), BF16),
        ((BLOCKS, BLK, FEAT), BF16),
        ((PAIRS, 2 * LINKS, BLK, 2 * WIDE), BF16),
        ((2, BLOCKS, BLK, WIDE), BF16),
        ((2, BLOCKS, BLK, WIDE), BF16),
        ((N_CTX, BLK, 2 * WIDE), BF16),
        ((N_CTX, BLK, 2 * WIDE), BF16),
        ((FRAMES, HALF), BF16),
        ((FEAT, HALF), BF16),
        ((FEAT, HALF), BF16),
        ((FRAMES, FEAT), F32),
        ((FRAMES, FEAT), BF16),
        ((FRAMES, FEAT), BF16),
        ((FRAMES, FEAT), BF16),
        ((FRAMES, FEAT), BF16),
        ((FRAMES + 2 * PAD, FEAT), BF16),
        ((FRAMES + 2 * PAD, FEAT), BF16),
        ((PH_ROWS, FEAT), BF16),
        ((PH_ROWS, FEAT), BF16),
        ((PH + 2 * PHC + PH_ROWS, FEAT), BF16),
        ((FRAMES + 2 * PAD, 2 * FEAT), F32),
        ((PH_ROWS, 2 * FEAT), F32),
        ((NONE + 1, BLK, 2 * WIDE), F32),
        ((PAIRS, 2 * LINKS, BLK, 2 * WIDE), BF16),
        ((KEYS, 2 * BLK), F32),
        ((KEYS, 2 * BLK), BF16),
        ((2 * BLK, 2 * BLK), F32),
        ((PH_ROWS, 2 * BLK), F32),
        ((PAIRS, LINKS + 1, BLK, 2 * WIDE), BF16),
        ((PAIRS, LINKS, BLK, 2 * WIDE), BF16),
        ((PAIRS, BLOCKS, BLK, 2 * WIDE), BF16),
        ((PAIRS, BLOCKS, BLK, 2 * WIDE), BF16),
        ((2, PAD, 2 * FEAT), BF16),
        ((2, PAD, 2 * FEAT), BF16),
        ((4, PHC, 2 * FEAT), BF16),
        ((4, PHC, 2 * FEAT), BF16),
        ((PHC, 2 * FEAT), BF16),
        ((2, OCT, PHC, 2 * FEAT), BF16),
        ((FRAMES, FEAT), BF16),
        ((FRAMES, FEAT), BF16),
        ((2, N_DP, OCT, SLAB, FEAT), BF16),
        ((N_DP, OCT, SLAB, FEAT), BF16),
        ((N_DP, OCT, SLAB, FEAT), BF16),
        ((N_DP - 1, OCT, SLAB, FEAT), BF16),
        ((OCT, SLAB, FEAT), BF16),
        ((OCT - 1, SLAB, FEAT), BF16),
        ((SLAB, FEAT), F32),
        ((SLAB, FEAT), F32),
    )
    return pl.pallas_call(
        layer_kernel,
        out_shape=(
            jax.ShapeDtypeStruct((FRAMES, HALF), BF16),
            jax.ShapeDtypeStruct((FRAMES, FEAT), BF16),
            jax.ShapeDtypeStruct((FRAMES, FEAT), BF16),
            jax.ShapeDtypeStruct((FRAMES, FEAT), BF16),
            jax.ShapeDtypeStruct((PH, FEAT), BF16),
            jax.ShapeDtypeStruct((PH, FEAT), BF16),
            jax.ShapeDtypeStruct((SLAB, FEAT), F32),
        ),
        in_specs=[SMEM, SMEM, VMEM, ANY, ANY, ANY, ANY, ANY, VMEM, VMEM],
        out_specs=(ANY,) * 7,
        scratch_shapes=[pltpu.VMEM(shape, kind) for shape, kind in scratch]
        + [
            pltpu.SemaphoreType.DMA((S_ALL,)),
            pltpu.SemaphoreType.DMA((S_ALL,)),
            pltpu.SemaphoreType.DMA((5 + 9,)),
        ],
        compiler_params=pltpu.CompilerParams(
            collective_id=0, has_side_effects=True, vmem_limit_bytes=BIG
        ),
        name="layer",
    )(
        tbl, count, align, k.reshape(BLOCKS, BLK, FEAT), v.reshape(BLOCKS, BLK, FEAT),
        q, cot, w, phk, phv,
    )


def hand_on_kernel(*refs):
    n = len(refs) // 2
    for i in range(n):
        refs[n + i][...] = refs[i][...]


def hand_on(*arrays):
    parts = 2
    specs = [pl.BlockSpec((a.shape[0] // parts, a.shape[1]), lambda i: (i, 0)) for a in arrays]
    return pl.pallas_call(
        hand_on_kernel,
        out_shape=tuple(jax.ShapeDtypeStruct(a.shape, a.dtype) for a in arrays),
        grid=(parts,),
        in_specs=specs,
        out_specs=tuple(specs),
        name="hand_on",
    )(*arrays)


def local(q, k, v, cot, w, phk, phv, tbl, count, align):
    q, k, v, cot, phk, phv, tbl = q[0], k[0], v[0], cot[0], phk[0], phv[0], tbl[0].T
    layer, dq, dk, dv, dphk, dphv, dw = layer_call(
        tbl, count, align, k, v, q, cot, w, phk, phv
    )
    layer, dq, dk, dv, dphk, dphv, dw = hand_on(layer, dq, dk, dv, dphk, dphv, dw)
    return (layer[None], dq[None], dk[None], dv[None], dphk[None], dphv[None], dw.T)


def solution(mesh):
    placed = (
        P("dp", "ctx", "head"),
        P("dp", "ctx", "head"),
        P("dp", "ctx", "head"),
        P("dp", "ctx", "head"),
        P("head", None),
        P("dp", None, "head"),
        P("dp", None, "head"),
        P("dp", None, None),
        P("dp", "ctx"),
        P("dp", "ctx"),
    )
    return jax.shard_map(
        local,
        mesh=mesh,
        in_specs=placed,
        out_specs=(
            P("dp", "ctx", "head"),
            P("dp", "ctx", "head"),
            P("dp", "ctx", "head"),
            P("dp", "ctx", "head"),
            P("dp", None, "head"),
            P("dp", None, "head"),
            P("head", ("ctx", "dp")),
        ),
        check_vma=False,
    )
```

```python
import functools
import math

import jax
import jax.numpy as jnp
from jax import lax
from jax.experimental import pallas as pl
from jax.experimental.pallas import tpu as pltpu
from jax.sharding import PartitionSpec as P

MESH = pl.DeviceIdType.MESH
ANY = pl.BlockSpec(memory_space=pl.ANY)
VMEM = pl.BlockSpec(memory_space=pltpu.VMEM)
SMEM = pl.BlockSpec(memory_space=pltpu.SMEM)
BF16 = jnp.bfloat16
F32 = jnp.float32

DH = 128
BLK = 128
HALF_BAND = 64
SLOTS = 4
PH_HALF = 16
PH = 256
N_CTX = 16
N_DP = 4
FRAMES = 512
BLOCKS = 4
FEAT = 512
MODEL = 2048
HALF = 1024
SEQ = FRAMES * N_CTX
PHC = 16
MASKED = -1e30
LOG2E = 1.4426950408889634
LINKS = 7
BIG = 60 * 1024 * 1024

NT = (((1,), (1,)), ((), ()))
NN = (((1,), (0,)), ((), ()))
TN = (((0,), (0,)), ((), ()))


def dot(a, b, dims):
    return lax.dot_general(a, b, dims, preferred_element_type=F32)


def flip_core(c):
    return c + 1 - 2 * (c % 2)


def flip_y(c):
    return c + 2 - 4 * ((c // 2) % 2)


def partner(me, j):
    if j == 0:
        return flip_core(me)
    hop, other = 1 + (j - 1) // 2, (j - 1) % 2
    low = me % 4
    low = flip_core(low) if other else low
    return ((me // 4 + hop) % 4) * 4 + low


def sender(me, j):
    if j == 0:
        return flip_core(me)
    hop, other = 1 + (j - 1) // 2, (j - 1) % 2
    low = me % 4
    low = flip_core(low) if other else low
    return ((me // 4 + 4 - hop) % 4) * 4 + low


ORDER = (3, 4, 1, 2, 5, 6, 0)


def named_block(tbl, user, owner):
    block, found = 0, 0
    for e in range(BLOCKS * SLOTS):
        entry = tbl[e % SLOTS, user * BLOCKS + e // SLOTS]
        hit = entry // BLOCKS == owner
        block = jnp.where(hit, entry % BLOCKS, block)
        found = jnp.where(hit, 1, found)
    return block, found


PAIRS = 2
WIDE = 2 * DH
PH_ROWS = 128
PAD = HALF_BAND
NONE = BLOCKS * SLOTS
SLAB = 32
OCT = N_CTX // 2
W_PART = FEAT // (2 * N_DP)
STEP = 16
EARLY = 3
KEYS = 6 * BLK + PH_ROWS

S_W, S_WG, S_AY, S_P, S_HALO, S_OWN, S_FWD = 0, 1, 8, 12, 13, 17, 31
S_R, S_D, S_Y, S_ATT, S_RIM, S_PHC, S_PHB, S_PHX = 45, 59, 73, 81, 83, 85, 89, 96
S_DWC, S_DWX, S_DWT, S_DWL, S_P1, S_DWC2, S_DWX2, S_ALL = 97, 98, 101, 108, 109, 110, 111, 114


def two_heads(x):
    zero = jnp.zeros((BLK, DH), x.dtype)
    top = jnp.concatenate([x[:, :DH], zero], axis=1)
    low = jnp.concatenate([zero, x[:, DH:]], axis=1)
    return jnp.concatenate([top, low], axis=0)


def layer_kernel(
    tbl, count, align, k_far, v_far, q, cot, w, phk, phv,
    layer_hbm, dq_hbm, dk_hbm, dv_hbm, dphk_hbm, dphv_hbm, dw_hbm,
    layer, dq, dk, dv, dphk, dphv, dw, k, v, ph_k, ph_v, stage, ay0, ay1, phr0, phr1, cot_v, w_m, w_o, part, p_out, p_in, grad, q_v, kpad, vpad, pk, pv, ph_tmp,
    dpad, dph, run, g, s_buf, p_buf, band_bias, ph_bias, s_buf2, p_buf2, band_bias2, ph_bias2, relayed, direct, rsum, summed,
    rims, rims_in, ph_out, ph_in, ph_mine, ph_all, att, att_o,
    dwx, dwc, dws, dwr, dwm, dwl, dwe, dwf, send, recv, near,
):
    ay, phr = (ay0, ay1), (phr0, phr1)
    me, head, lane = lax.axis_index("ctx"), lax.axis_index("head"), lax.axis_index("dp")
    across, twin = flip_y(me), flip_core(me)
    prev, nxt = (me + N_CTX - 1) % N_CTX, (me + 1) % N_CTX
    parity = me % 2
    first = me * FRAMES
    mine = pl.ds(pl.multiple_of(head * HALF, HALF), HALF)
    theirs = pl.ds(pl.multiple_of((1 - head) * HALF, HALF), HALF)
    mesh_peers = [{"ctx": (me + s) % N_CTX} for s in range(1, N_CTX)]
    mesh_peers += [{"dp": (lane + s) % N_DP} for s in range(1, N_DP)]
    mesh_peers += [{"head": 1 - head}, {"ctx": (me + OCT) % N_CTX, "head": 1 - head}]
    barrier = pltpu.get_barrier_semaphore()
    for device in mesh_peers:
        pl.semaphore_signal(barrier, inc=1, device_id=device, device_id_type=MESH)
    loads = [
        pltpu.make_async_copy(cot, cot_v, near.at[0]),
        pltpu.make_async_copy(w.at[:, mine], w_m, near.at[1]),
        pltpu.make_async_copy(q, q_v, near.at[2]),
    ]
    kv_loads = [
        pltpu.make_async_copy(k_far, k, near.at[3]),
        pltpu.make_async_copy(v_far, v, near.at[4]),
    ]
    ph_loads = [
        pltpu.make_async_copy(phk, ph_k, near.at[14]),
        pltpu.make_async_copy(phv, ph_v, near.at[15]),
    ]
    for c in kv_loads + loads + ph_loads:
        c.start()

    results = []

    def deliver(src, dst):
        c = pltpu.make_async_copy(src, dst, near.at[5 + len(results)])
        c.start()
        results.append(c)

    def remote(i, src, dst, **to):
        c = pltpu.make_async_remote_copy(
            src, dst, send.at[i], recv.at[i], device_id=to, device_id_type=MESH
        )
        c.start()
        return c

    own_block = {j: named_block(tbl, partner(me, j), me)[0] for j in ORDER}
    far_block = {j: named_block(tbl, partner(me, j), across)[0] for j in ORDER}
    far_block[LINKS] = named_block(tbl, me, across)[0]
    pl.semaphore_wait(barrier, len(mesh_peers))

    def eighth(of):
        return w_o.at[pl.ds(pl.multiple_of((of * 2 + parity) * W_PART, W_PART), W_PART)]

    w_rows = pl.ds(pl.multiple_of((lane * 2 + parity) * W_PART, W_PART), W_PART)
    w_first = remote(S_W, w.at[w_rows, theirs], eighth(lane), head=1 - head)

    def across_copy(p, n):
        lanes = pl.ds(p * WIDE, WIDE)
        src = (k_far, v_far)[n]
        return remote(S_AY + 2 * p + n, src.at[:, :, lanes], ay[p].at[n], ctx=across)

    ay_copies = [[across_copy(0, 0)], []]
    kv_copies = [[], []]

    def send_own(p, these=ORDER):
        for j in these:
            lanes = slice(p * WIDE, (p + 1) * WIDE)
            stage[p, j, :, :WIDE] = k[own_block[j], :, lanes]
            stage[p, j, :, WIDE:] = v[own_block[j], :, lanes]
            kv_copies[p].append(
                remote(S_OWN + LINKS * p + j, stage.at[p, j], phr[p].at[me], ctx=partner(me, j))
            )

    def send_far(p):
        for j in ORDER:
            stage[p, LINKS + j, :, :WIDE] = ay[p][0, far_block[j]]
            stage[p, LINKS + j, :, WIDE:] = ay[p][1, far_block[j]]
            kv_copies[p].append(
                remote(
                    S_FWD + LINKS * p + j, stage.at[p, LINKS + j], phr[p].at[across],
                    ctx=partner(me, j),
                )
            )
        phr[p][across, :, :WIDE] = ay[p][0, far_block[LINKS]]
        phr[p][across, :, WIDE:] = ay[p][1, far_block[LINKS]]

    for c in kv_loads:
        c.wait()
    send_own(0)
    w_first.wait()
    w_x = [remote(S_WG + s - 1, eighth(lane), eighth(lane), dp=(lane + s) % N_DP) for s in range(1, N_DP)]
    w_core = [remote(S_WG + N_DP - 1, eighth(lane), eighth(lane), ctx=twin)]
    ay_copies[0].append(across_copy(0, 1))
    tail = pl.ds(BLK - PAD, PAD)
    halo_copies = []
    for n, (src, dst) in enumerate(((k_far, kpad), (v_far, vpad))):
        halo_copies += [
            remote(S_HALO + n, src.at[BLOCKS - 1, tail], dst.at[pl.ds(0, PAD)], ctx=nxt),
            remote(
                S_HALO + 2 + n, src.at[0, pl.ds(0, PAD)], dst.at[pl.ds(PAD + FRAMES, PAD)],
                ctx=prev,
            ),
        ]
    send_own(1, ORDER[:EARLY])
    for pad, src in ((kpad, k), (vpad, v)):
        for b in range(BLOCKS):
            pad[PAD + b * BLK : PAD + (b + 1) * BLK, :] = src[b]
    for c in ph_loads:
        c.wait()
    for dst, src in ((pk, ph_k), (pv, ph_v)):
        ph_tmp[...] = jnp.zeros_like(ph_tmp)
        ph_tmp[2 * PHC : 2 * PHC + PH, :] = src[...]
        dst[...] = ph_tmp[pl.ds(pl.multiple_of(me * PHC, PHC), PH_ROWS), :]
    dpad[...] = jnp.zeros_like(dpad)
    dph[...] = jnp.zeros_like(dph)
    run[NONE] = jnp.zeros((BLK, 2 * WIDE), F32)
    for c in loads:
        c.wait()

    def each_block(body):
        def step(i, _):
            body(pl.ds(pl.multiple_of(i * BLK, BLK), BLK))
            return 0

        lax.fori_loop(0, BLOCKS, step, 0)

    def own_part(rows):
        part[rows, :] = dot(cot_v[rows, :], w_m[...], NT)

    each_block(own_part)
    for n in range(1, N_DP):
        w_x[n - 1].wait()
        came = eighth((lane + N_DP - n) % N_DP)
        w_core.append(remote(S_WG + N_DP - 1 + n, came, came, ctx=twin))
    for c in ay_copies[0]:
        c.wait()
    ay_copies[1] = [across_copy(1, 0), across_copy(1, 1)]
    send_far(0)
    for c in w_core:
        c.wait()

    def other_part(p):
        lanes = slice(p * WIDE, (p + 1) * WIDE)

        def step(rows):
            p_out[rows, lanes] = dot(cot_v[rows, :], w_o[lanes, :], NT).astype(BF16)

        each_block(step)

    def send_part(p):
        lanes = pl.ds(p * WIDE, WIDE)
        return remote((S_P, S_P1)[p], p_out.at[:, lanes], p_in.at[:, lanes], head=1 - head)

    other_part(0)
    p_copies = [send_part(0)]
    send_own(1, ORDER[EARLY:])
    other_part(1)
    for c in ay_copies[1]:
        c.wait()
    send_far(1)
    p_copies.append(send_part(1))

    def whole_grad(p):
        lanes = slice(p * WIDE, (p + 1) * WIDE)
        p_copies[p].wait()

        def step(rows):
            grad[rows, lanes] = (part[rows, lanes] + p_in[rows, lanes].astype(F32)).astype(BF16)

        each_block(step)

    whole_grad(0)
    for c in halo_copies:
        c.wait()

    rate = DH ** (-0.5)
    sources = [tbl[e % SLOTS, me * BLOCKS + e // SLOTS] // BLOCKS for e in range(NONE)]

    def attend(p):
        lanes = slice(p * WIDE, (p + 1) * WIDE)
        klanes = slice(p * 2 * WIDE, p * 2 * WIDE + WIDE)
        vlanes = slice(p * 2 * WIDE + WIDE, (p + 1) * 2 * WIDE)

        def block(i, s_buf, p_buf, band_bias, ph_bias):
            rows = pl.ds(pl.multiple_of(i * BLK, BLK), BLK)
            wide = pl.ds(pl.multiple_of(i * BLK, BLK), 2 * BLK)
            row = lax.broadcasted_iota(jnp.int32, (2 * BLK, BLK), 0)
            col = lax.broadcasted_iota(jnp.int32, (2 * BLK, BLK), 1)
            pos = first + i * BLK - PAD + row
            seen = (jnp.abs(col - row + PAD) <= HALF_BAND) & (pos >= 0) & (pos < SEQ)
            bias = jnp.where(seen, 0.0, MASKED).astype(F32)
            band_bias[...] = jnp.concatenate([bias, bias], axis=1)
            phone = me * PHC - 2 * PHC + lax.broadcasted_iota(jnp.int32, (PH_ROWS, BLK), 0)
            near_by = jnp.abs(phone - align[0:1, rows]) <= PH_HALF
            near_by = near_by & (phone >= 0) & (phone < PH)
            bias = jnp.where(near_by, 0.0, MASKED).astype(F32)
            ph_bias[...] = jnp.concatenate([bias, bias], axis=1)
            n_used = count[0, i]
            named = [tbl[n, me * BLOCKS + i] // BLOCKS for n in range(SLOTS)]
            slot_bias = [jnp.where(n < n_used, 0.0, MASKED).astype(F32) for n in range(SLOTS)]
            qbd = two_heads(q_v[rows, lanes])
            g2 = grad[rows, lanes]
            gbd = two_heads(g2)

            def keys(c, side):
                own_pad, ph_win = ((kpad, pk), (vpad, pv))[side]
                where = slice(side * WIDE, (side + 1) * WIDE)
                if c == 0:
                    return own_pad[wide, lanes]
                if c == 3:
                    return ph_win[:, lanes]
                return jnp.concatenate(
                    [phr[p][named[2 * c - 2], :, where], phr[p][named[2 * c - 1], :, where]], axis=0
                )

            sizes = (2 * BLK, 2 * BLK, 2 * BLK, PH_ROWS)
            start = (0, 2 * BLK, 4 * BLK, 6 * BLK)
            top = jnp.full((1, 2 * BLK), -3e38, F32)
            for c in range(4):
                s = dot(keys(c, 0), qbd, NT) * (rate * LOG2E)
                if c == 0:
                    s = s + band_bias[...]
                elif c == 3:
                    s = s + ph_bias[...]
                else:
                    s = jnp.concatenate(
                        [s[:BLK] + slot_bias[2 * c - 2], s[BLK:] + slot_bias[2 * c - 1]], axis=0
                    )
                s_buf[start[c] : start[c] + sizes[c], :] = s
                top = jnp.maximum(top, jnp.max(s, axis=0, keepdims=True))
            total = jnp.zeros((1, 2 * BLK), F32)
            for c in range(4):
                at = slice(start[c], start[c] + sizes[c])
                e = jnp.exp2(s_buf[at, :] - top)
                s_buf[at, :] = e
                total = total + jnp.sum(e, axis=0, keepdims=True)
            inverse = 1.0 / total
            mixed = jnp.zeros((2 * BLK, WIDE), F32)
            for c in range(4):
                at = slice(start[c], start[c] + sizes[c])
                prob = s_buf[at, :] * inverse
                s_buf[at, :] = prob
                half = prob.astype(BF16)
                p_buf[at, :] = half
                mixed = mixed + dot(half, keys(c, 1), TN)
            a2 = jnp.concatenate([mixed[:BLK, :DH], mixed[BLK:, DH:]], axis=1).astype(BF16)
            att[rows, lanes] = a2
            product = g2.astype(F32) * a2.astype(F32)
            delta = jnp.concatenate(
                [
                    jnp.sum(product[:, :DH].T, axis=0, keepdims=True),
                    jnp.sum(product[:, DH:].T, axis=0, keepdims=True),
                ],
                axis=1,
            )
            dq2 = jnp.zeros((2 * BLK, WIDE), F32)
            for c in range(4):
                at = slice(start[c], start[c] + sizes[c])
                d_weight = dot(keys(c, 1), gbd, NT)
                ds = (s_buf[at, :] * (d_weight - delta) * rate).astype(BF16)
                dq2 = dq2 + dot(ds, keys(c, 0), TN)
                dk2 = dot(ds, qbd, NN)
                dv2 = dot(p_buf[at, :], gbd, NN)
                if c == 0:
                    dpad[wide, klanes] += dk2
                    dpad[wide, vlanes] += dv2
                elif c == 3:
                    dph[:, klanes] += dk2
                    dph[:, vlanes] += dv2
                else:
                    for n in range(2):
                        slot = 2 * c - 2 + n
                        here = i * SLOTS + slot
                        before = NONE
                        for e in range(NONE):
                            same = (sources[e] == named[slot]) & (here > e)
                            before = jnp.where(same, e, before)
                        half_rows = slice(n * BLK, (n + 1) * BLK)
                        run[here, :, :WIDE] = dk2[half_rows] + run[before, :, :WIDE]
                        run[here, :, WIDE:] = dv2[half_rows] + run[before, :, WIDE:]
            dq[rows, lanes] = jnp.concatenate([dq2[:BLK, :DH], dq2[BLK:, DH:]], axis=1).astype(BF16)

        def two_blocks(n, _):
            block(2 * n, s_buf, p_buf, band_bias, ph_bias)
            block(2 * n + 1, s_buf2, p_buf2, band_bias2, ph_bias2)
            return 0

        lax.fori_loop(0, BLOCKS // 2, two_blocks, 0)

    def grads_of(owner):
        last = NONE
        for e in range(NONE):
            last = jnp.where(sources[e] == owner, e, last)
        return run[last].astype(BF16)

    to_relay, straight, att_copies = [{}, {}], [{}, {}], []

    def collect(p):
        lanes = pl.ds(p * WIDE, WIDE)
        att_copies.append(
            remote(S_ATT + p, att.at[:, lanes], att_o.at[:, lanes], head=1 - head)
        )
        for j in ORDER:
            to = partner(me, j)
            g[p, j] = grads_of(flip_y(to))
            to_relay[p][j] = remote(
                S_R + LINKS * p + j, g.at[p, j], relayed.at[p, j], ctx=to
            )
        relayed[p, LINKS] = grads_of(across)
        for j in ORDER:
            g[p, LINKS + j] = grads_of(partner(me, j))

    def send_straight(p):
        for j in ORDER:
            straight[p][j] = remote(
                S_D + LINKS * p + j, g.at[p, LINKS + j], direct.at[p, j], ctx=partner(me, j)
            )

    def slabs(features, side, lanes=slice(0, FEAT)):
        def step(n, _):
            cols = pl.ds(pl.multiple_of(n * BLK, BLK), BLK)
            piece = dot(cot_v[:, cols], features[:, lanes], TN).astype(BF16)
            at = side * (OCT // 2) + n // 2
            for d in range(N_DP):
                dwx[n % 2, d, at, :, lanes] = piece[d * SLAB : (d + 1) * SLAB]
            return 0

        lax.fori_loop(0, OCT, step, 0)

    for c in kv_copies[0]:
        c.wait()
    attend(0)
    collect(0)
    slabs(att, head, slice(0, WIDE))
    whole_grad(1)
    for c in kv_copies[1]:
        c.wait()
    send_straight(0)
    attend(1)
    collect(1)
    deliver(dq, dq_hbm)
    def to_core(side, second):
        part_of = pl.ds(pl.multiple_of(side * (OCT // 2), OCT // 2), OCT // 2)
        return remote(
            (S_DWC, S_DWC2)[second], dwx.at[1 - parity, :, part_of], dwc.at[:, part_of], ctx=twin
        )

    dw_x = []

    def to_dp(side, second, core):
        core.wait()

        def over_core(n, _):
            i = side * (OCT // 2) + n
            for d in range(N_DP):
                dws[d, i] = (dwx[parity, d, i].astype(F32) + dwc[d, i].astype(F32)).astype(BF16)
            return 0

        lax.fori_loop(0, OCT // 2, over_core, 0)
        part_of = pl.ds(pl.multiple_of(side * (OCT // 2), OCT // 2), OCT // 2)
        for n in range(1, N_DP):
            to = (lane + n) % N_DP
            dw_x.append(
                remote(
                    (S_DWX, S_DWX2)[second] + n - 1, dws.at[to, part_of], dwr.at[n - 1, part_of],
                    dp=to,
                )
            )

    slabs(att, head, slice(WIDE, FEAT))
    core_own = to_core(head, 0)
    rims[0] = dpad[:PAD, :].astype(BF16)
    rims[1] = dpad[PAD + FRAMES :, :].astype(BF16)
    rim_copies = [
        remote(S_RIM, rims.at[0], rims_in.at[0], ctx=prev),
        remote(S_RIM + 1, rims.at[1], rims_in.at[1], ctx=nxt),
    ]
    ph_copies = []
    for n, (chunk, by) in enumerate(((0, -2), (1, -1), (3, 1), (4, 2))):
        ph_out[n] = dph[chunk * PHC : (chunk + 1) * PHC, :].astype(BF16)
        ph_copies.append(remote(S_PHC + n, ph_out.at[n], ph_in.at[n], ctx=(me + N_CTX + by) % N_CTX))

    weights_far, weights_own = [], []
    for u in [sender(me, j) for j in range(LINKS)] + [me]:
        for owner, weights in ((across, weights_far), (me, weights_own)):
            block, found = named_block(tbl, u, owner)
            weights.append(
                [jnp.where((block == b) & (found == 1), 1.0, 0.0).astype(F32) for b in range(BLOCKS)]
            )
    relay_copies = [[], []]

    def relay(p):
        for j in ORDER:
            to_relay[p][j].wait()
        for b in range(BLOCKS):

            def add(i, _, b=b):
                rows = pl.ds(pl.multiple_of(i * STEP, STEP), STEP)
                t = relayed[p, 0, rows, :].astype(F32) * weights_far[0][b]
                for n in range(1, LINKS + 1):
                    t = t + relayed[p, n, rows, :].astype(F32) * weights_far[n][b]
                rsum[p, b, rows, :] = t.astype(BF16)
                return 0

            lax.fori_loop(0, BLK // STEP, add, 0)
            relay_copies[p].append(
                remote(S_Y + BLOCKS * p + b, rsum.at[p, b], summed.at[p, b], ctx=across)
            )

    relay(0)
    send_straight(1)
    to_dp(head, 0, core_own)
    for c in att_copies:
        c.wait()
    slabs(att_o, 1 - head)
    core_other = to_core(1 - head, 1)

    for c in ph_copies:
        c.wait()
    total = dph[2 * PHC : 3 * PHC, :]
    for n, by in ((0, 2), (1, 1), (2, -1), (3, -2)):
        origin = me + by
        there = (origin >= 0) & (origin < N_CTX)
        total = total + jnp.where(there, ph_in[n].astype(F32), 0.0)
    ph_mine[...] = total.astype(BF16)
    ph_all[parity, me // 2] = ph_mine[...]
    ph_bcast = [
        remote(S_PHB + s - 1, ph_mine, ph_all.at[parity, me // 2], ctx=(me + 2 * s) % N_CTX)
        for s in range(1, OCT)
    ]
    relay(1)
    to_dp(1 - head, 1, core_other)

    def project(rows):
        t = dot(att[rows, :], w_m[...], NN) + dot(att_o[rows, :], w_o[...], NN)
        layer[rows, :] = t.astype(BF16)

    each_block(project)
    deliver(layer, layer_hbm)
    for c in dw_x:
        c.wait()

    def over_dp(i, _):
        t = dws[lane, i].astype(F32)
        for s in range(N_DP - 1):
            t = t + dwr[s, i].astype(F32)
        dwm[i] = t.astype(BF16)
        return 0

    lax.fori_loop(0, OCT, over_dp, 0)
    dw_t = []
    for s in range(1, OCT):
        to = (me + 2 * s) % N_CTX
        dw_t.append(remote(S_DWT + s - 1, dwm.at[to // 2], dwl.at[s - 1], ctx=to))

    for c in dw_t:
        c.wait()
    t = dwm[me // 2].astype(F32)
    for s in range(OCT - 1):
        t = t + dwl[s].astype(F32)
    dwe[...] = t * (1.0 / math.sqrt(N_DP * SEQ))
    dw_last = remote(S_DWL, dwe, dwf, ctx=(me + OCT) % N_CTX, head=1 - head)
    for c in ph_bcast:
        c.wait()
    ph_core = remote(S_PHX, ph_all.at[parity], ph_all.at[parity], ctx=twin)
    def finish(p):
        for j in ORDER:
            straight[p][j].wait()
        lanes = slice(p * WIDE, (p + 1) * WIDE)
        both = slice(p * 2 * WIDE, (p + 1) * 2 * WIDE)
        for b in range(BLOCKS):
            relay_copies[p][b].wait()

            def add(i, _, b=b):
                rows = pl.ds(pl.multiple_of(i * STEP, STEP), STEP)
                here = pl.ds(pl.multiple_of(b * BLK + i * STEP, STEP), STEP)
                there = pl.ds(pl.multiple_of(PAD + b * BLK + i * STEP, STEP), STEP)
                t = dpad[there, both] + summed[p, b, rows, :].astype(F32)
                for n in range(LINKS):
                    t = t + direct[p, n, rows, :].astype(F32) * weights_own[n][b]
                dk[here, lanes] = t[:, :WIDE].astype(BF16)
                dv[here, lanes] = t[:, WIDE:].astype(BF16)
                return 0

            lax.fori_loop(0, BLK // STEP, add, 0)
        some = pl.ds(p * WIDE, WIDE)
        deliver(dk.at[:, some], dk_hbm.at[:, some])
        deliver(dv.at[:, some], dv_hbm.at[:, some])

    for c in rim_copies:
        c.wait()
    low, high = slice(PAD, 2 * PAD), slice(FRAMES, FRAMES + PAD)
    dpad[high, :] += jnp.where(me < N_CTX - 1, rims_in[0].astype(F32), 0.0)
    dpad[low, :] += jnp.where(me > 0, rims_in[1].astype(F32), 0.0)
    finish(0)
    ph_core.wait()
    for i in range(N_CTX):
        at = slice(i * PHC, (i + 1) * PHC)
        for p in range(PAIRS):
            lanes = slice(p * WIDE, (p + 1) * WIDE)
            here = p * 2 * WIDE
            dphk[at, lanes] = ph_all[i % 2, i // 2, :, here : here + WIDE]
            dphv[at, lanes] = ph_all[i % 2, i // 2, :, here + WIDE : here + 2 * WIDE]
    deliver(dphk, dphk_hbm)
    deliver(dphv, dphv_hbm)
    finish(1)
    dw_last.wait()
    dw[...] = jnp.where(me // OCT == head, dwe[...], dwf[...])
    deliver(dw, dw_hbm)
    for c in results:
        c.wait()


def layer_call(tbl, count, align, k, v, q, cot, w, phk, phv):
    scratch = (
        ((FRAMES, HALF), BF16),
        ((FRAMES, FEAT), BF16),
        ((FRAMES, FEAT), BF16),
        ((FRAMES, FEAT), BF16),
        ((PH, FEAT), BF16),
        ((PH, FEAT), BF16),
        ((SLAB, FEAT), F32),
        ((BLOCKS, BLK, FEAT), BF16),
        ((BLOCKS, BLK, FEAT), BF16),
        ((PH, FEAT), BF16),
        ((PH, FEAT), BF16),
        ((PAIRS, 2 * LINKS, BLK, 2 * WIDE), BF16),
        ((2, BLOCKS, BLK, WIDE), BF16),
        ((2, BLOCKS, BLK, WIDE), BF16),
        ((N_CTX, BLK, 2 * WIDE), BF16),
        ((N_CTX, BLK, 2 * WIDE), BF16),
        ((FRAMES, HALF), BF16),
        ((FEAT, HALF), BF16),
        ((FEAT, HALF), BF16),
        ((FRAMES, FEAT), F32),
        ((FRAMES, FEAT), BF16),
        ((FRAMES, FEAT), BF16),
        ((FRAMES, FEAT), BF16),
        ((FRAMES, FEAT), BF16),
        ((FRAMES + 2 * PAD, FEAT), BF16),
        ((FRAMES + 2 * PAD, FEAT), BF16),
        ((PH_ROWS, FEAT), BF16),
        ((PH_ROWS, FEAT), BF16),
        ((PH + 2 * PHC + PH_ROWS, FEAT), BF16),
        ((FRAMES + 2 * PAD, 2 * FEAT), F32),
        ((PH_ROWS, 2 * FEAT), F32),
        ((NONE + 1, BLK, 2 * WIDE), F32),
        ((PAIRS, 2 * LINKS, BLK, 2 * WIDE), BF16),
        ((KEYS, 2 * BLK), F32),
        ((KEYS, 2 * BLK), BF16),
        ((2 * BLK, 2 * BLK), F32),
        ((PH_ROWS, 2 * BLK), F32),
        ((KEYS, 2 * BLK), F32),
        ((KEYS, 2 * BLK), BF16),
        ((2 * BLK, 2 * BLK), F32),
        ((PH_ROWS, 2 * BLK), F32),
        ((PAIRS, LINKS + 1, BLK, 2 * WIDE), BF16),
        ((PAIRS, LINKS, BLK, 2 * WIDE), BF16),
        ((PAIRS, BLOCKS, BLK, 2 * WIDE), BF16),
        ((PAIRS, BLOCKS, BLK, 2 * WIDE), BF16),
        ((2, PAD, 2 * FEAT), BF16),
        ((2, PAD, 2 * FEAT), BF16),
        ((4, PHC, 2 * FEAT), BF16),
        ((4, PHC, 2 * FEAT), BF16),
        ((PHC, 2 * FEAT), BF16),
        ((2, OCT, PHC, 2 * FEAT), BF16),
        ((FRAMES, FEAT), BF16),
        ((FRAMES, FEAT), BF16),
        ((2, N_DP, OCT, SLAB, FEAT), BF16),
        ((N_DP, OCT, SLAB, FEAT), BF16),
        ((N_DP, OCT, SLAB, FEAT), BF16),
        ((N_DP - 1, OCT, SLAB, FEAT), BF16),
        ((OCT, SLAB, FEAT), BF16),
        ((OCT - 1, SLAB, FEAT), BF16),
        ((SLAB, FEAT), F32),
        ((SLAB, FEAT), F32),
    )
    return pl.pallas_call(
        layer_kernel,
        out_shape=(
            jax.ShapeDtypeStruct((FRAMES, HALF), BF16),
            jax.ShapeDtypeStruct((FRAMES, FEAT), BF16),
            jax.ShapeDtypeStruct((FRAMES, FEAT), BF16),
            jax.ShapeDtypeStruct((FRAMES, FEAT), BF16),
            jax.ShapeDtypeStruct((PH, FEAT), BF16),
            jax.ShapeDtypeStruct((PH, FEAT), BF16),
            jax.ShapeDtypeStruct((SLAB, FEAT), F32),
        ),
        in_specs=[SMEM, SMEM, VMEM] + [ANY] * 7,
        out_specs=(ANY,) * 7,
        scratch_shapes=[pltpu.VMEM(shape, kind) for shape, kind in scratch]
        + [
            pltpu.SemaphoreType.DMA((S_ALL,)),
            pltpu.SemaphoreType.DMA((S_ALL,)),
            pltpu.SemaphoreType.DMA((16,)),
        ],
        compiler_params=pltpu.CompilerParams(
            collective_id=0, has_side_effects=True, vmem_limit_bytes=BIG
        ),
        name="layer",
    )(
        tbl, count, align, k.reshape(BLOCKS, BLK, FEAT), v.reshape(BLOCKS, BLK, FEAT),
        q, cot, w, phk, phv,
    )


def hand_on_kernel(*refs):
    n = len(refs) // 2
    for i in range(n):
        refs[n + i][...] = refs[i][...]


def hand_on(*arrays):
    parts = 2
    specs = [pl.BlockSpec((a.shape[0] // parts, a.shape[1]), lambda i: (i, 0)) for a in arrays]
    return pl.pallas_call(
        hand_on_kernel,
        out_shape=tuple(jax.ShapeDtypeStruct(a.shape, a.dtype) for a in arrays),
        grid=(parts,),
        in_specs=specs,
        out_specs=tuple(specs),
        name="hand_on",
    )(*arrays)


def local(q, k, v, cot, w, phk, phv, tbl, count, align):
    q, k, v, cot, phk, phv, tbl = q[0], k[0], v[0], cot[0], phk[0], phv[0], tbl[0].T
    layer, dq, dk, dv, dphk, dphv, dw = layer_call(
        tbl, count, align, k, v, q, cot, w, phk, phv
    )
    layer, dq, dk, dv, dphk, dphv, dw = hand_on(layer, dq, dk, dv, dphk, dphv, dw)
    return (layer[None], dq[None], dk[None], dv[None], dphk[None], dphv[None], dw.T)


def solution(mesh):
    placed = (
        P("dp", "ctx", "head"),
        P("dp", "ctx", "head"),
        P("dp", "ctx", "head"),
        P("dp", "ctx", "head"),
        P("head", None),
        P("dp", None, "head"),
        P("dp", None, "head"),
        P("dp", None, None),
        P("dp", "ctx"),
        P("dp", "ctx"),
    )
    return jax.shard_map(
        local,
        mesh=mesh,
        in_specs=placed,
        out_specs=(
            P("dp", "ctx", "head"),
            P("dp", "ctx", "head"),
            P("dp", "ctx", "head"),
            P("dp", "ctx", "head"),
            P("dp", None, "head"),
            P("dp", None, "head"),
            P("head", ("ctx", "dp")),
        ),
        check_vma=False,
    )
```
